256 devices in a mesh: grp: 16 (over x, y), beam: 16 (over z, core).
Axes of the slice: x: 4, y: 4, z: 8, core: 2. Of those that a mesh axis runs over, the one named last changes fastest.
Arguments:
- subimages: float32 [2, 16, 2048, 2048], P(None, 'grp', 'beam'), may hold values from -6 to 6
- beam_weights: float32 [2, 2, 2, 4], replicated, may hold values from -3 to 3
- range_tiles: float32 [2, 3, 512, 512], replicated, may hold values from -0.15625 to 0.15625
- tile_offsets: int32 [2, 2, 128], P(None, None, 'beam'), may hold values from 0 to 2
- phase_rates: float32 [2, 2, 2048], P(None, None, 'beam'), may hold values from -3 to 3
Outputs:
- merged: float32 [2, 16, 2048, 2048], P(None, 'grp', 'beam')
The draws below stay inside these ranges and needn't reach their ends.
All inputs are finite; a program needn't handle non-finite values.
Results may differ from the reference program's by a relative error of at most 0.0001.
Values sent between devices are 32-bit elements; how exact they have to be, the bound alone decides.
No kernel may reach another device: no remote copies, remote signals or barrier semaphores. Data moves between devices by JAX's collectives and lax.ppermute only.
A program may use at most 128 MiB of HBM per device.

```python
import jax
import jax.numpy as jnp
from jax import lax

RBINS = 2048
TILE = 512
TAPS = 3
BLK = 16
MERGES = 2
BIT1 = 0
BIT2 = 1
GROUPS = 16
BEAMS = 2048
NBLK = 128


def place_ends(drawn, stream_key, smallest, high):
    longest = drawn.shape.index(max(drawn.shape))
    spots = []
    for shift in (0, 1):
        where = [jax.random.randint(jax.random.fold_in(stream_key, axis), (), 0, length) for axis, length in enumerate(drawn.shape)]
        where[longest] = (where[longest] + shift) % drawn.shape[longest]
        spots.append(tuple(where))
    return drawn.at[spots[0]].set(smallest).at[spots[1]].set(high)


def block_levels(own_key, dims, pieces, least, top_value):
    def one(dim, parts):
        heights = jax.random.uniform(jax.random.fold_in(jax.random.fold_in(own_key, 6), dim), (parts,), jnp.float32, least / len(pieces), top_value / len(pieces))
        return jnp.repeat(jnp.exp(heights), dims[dim] // parts).reshape((-1,) + (1,) * (len(dims) - dim - 1))

    loudness = one(*pieces[0])
    for cut in pieces[1:]:
        loudness = loudness * one(*cut)
    return loudness


def normal_values(rng, extent, scale, limit, shards=(), held_as=jnp.bfloat16):
    values = jax.random.normal(rng, extent, jnp.float32) * scale
    if len(shards) > 0:
        values = block_levels(rng, extent, shards, -0.22, 0.18) * values
    return jnp.clip(values, min=-limit, max=limit).astype(held_as)


def setup_inputs(seed: int = 0) -> dict:
    key_of = jax.random.split(jax.random.key(seed), 6)
    return {
        "subimages": normal_values(key_of[0], (2, GROUPS, BEAMS, RBINS), 1.0, 6.0, ((1, 16), (2, 16)), jnp.float32),
        "beam_weights": normal_values(key_of[1], (MERGES, 2, 2, 4), 0.5, 3.0, (), jnp.float32),
        "range_tiles": normal_values(key_of[2], (MERGES, TAPS, TILE, TILE), (TAPS * TILE) ** -0.5, 0.15625, (), jnp.float32),
        "tile_offsets": place_ends(jax.random.randint(key_of[3], (MERGES, 2, NBLK), 0, 3), jax.random.fold_in(key_of[3], 1), 0, 2).astype(jnp.int32),
        "phase_rates": jnp.clip(jax.random.uniform(key_of[4], (MERGES, 2, BEAMS), jnp.float32, -3.0, 3.0) * block_levels(key_of[4], (MERGES, 2, BEAMS), ((2, 16),), -0.4, 0.0), -3.0, 3.0),
    }


def range_interp(rows, offsets, tiles):
    beams_here = rows.shape[1]
    width = rows.shape[2]
    padded = jnp.pad(rows, ((0, 0), (0, 0), (TILE, 3 * TILE)))

    def block_step(block_index, result):
        rows_block = lax.dynamic_slice_in_dim(padded, (block_index * BLK).astype(jnp.int32), BLK, 1)
        shift_tiles = offsets[block_index].astype(jnp.int32)
        summed = jnp.zeros((2, BLK, width // TILE, TILE), rows.dtype)
        for tap_no in range(TAPS):
            window = lax.dynamic_slice_in_dim(rows_block, ((shift_tiles + tap_no) * TILE).astype(jnp.int32), width, 2)
            window = window.reshape(2, BLK, width // TILE, TILE)
            summed = summed + jnp.einsum("cbnt,tu->cbnu", window, tiles[tap_no], precision=lax.Precision.HIGHEST)
        return lax.dynamic_update_slice_in_dim(result, summed.reshape(2, BLK, width), (block_index * BLK).astype(jnp.int32), 1)

    result = jnp.zeros((2, beams_here, width), rows.dtype)
    return lax.fori_loop(jnp.int32(0), jnp.int32(beams_here // BLK), block_step, result)


def contribute(rimmed, section_no, parity_out, child_bit, beam_weights, range_tiles, tile_offsets, phase_rates):
    beams_here = rimmed.shape[1] - 4
    width = rimmed.shape[2]
    weights = beam_weights[section_no][parity_out, child_bit]
    blended = weights[0] * rimmed[:, 1:1 + beams_here]
    for beam_tap in range(1, 4):
        blended = blended + weights[beam_tap] * rimmed[:, 1 + beam_tap:1 + beam_tap + beams_here]
    ranged = range_interp(blended, tile_offsets[section_no][child_bit], range_tiles[section_no])
    column_pos = jnp.arange(width).astype(rimmed.dtype) / TILE
    angles = phase_rates[section_no][child_bit][:, None] * column_pos[None, :]
    cosine = jnp.cos(angles)
    sine_part = jnp.sin(angles)
    real_part = ranged[0] * cosine - ranged[1] * sine_part
    imag_part = ranged[0] * sine_part + ranged[1] * cosine
    return jnp.stack((real_part, imag_part))


def reference(subimages, beam_weights, range_tiles, tile_offsets, phase_rates):
    current = subimages
    for section_no, bit_pos in ((0, BIT1), (1, BIT2)):
        padded = jnp.pad(current, ((0, 0), (0, 0), (2, 2), (0, 0)))
        results = []
        for group_no in range(GROUPS):
            parity = (group_no >> bit_pos) & 1
            total = None
            for child_bit in (0, 1):
                source = group_no - (parity << bit_pos) + (child_bit << bit_pos)
                term = contribute(padded[:, source], section_no, parity, child_bit, beam_weights, range_tiles, tile_offsets, phase_rates)
                total = term if total is None else total + term
            results.append(total)
        current = jnp.stack(results, axis=1)
    return current
```

```python
import functools

import jax
import jax.numpy as jnp
from jax import lax
from jax.experimental import pallas as pl
from jax.experimental.pallas import tpu as pltpu
from jax.sharding import PartitionSpec as P

TILE = 512
TAPS = 3
BLK = 16
RING = 4
QROWS = 32
EDGE = 8
ROWS = QROWS + EDGE
WIDTH = 2048
TILES = WIDTH // TILE
FULL = WIDTH + 2 * TILE
LANES = 256
SPANS = ((0, 16), (16, 32), (32, 40))
HBM = pl.BlockSpec(memory_space=pl.ANY)
VMEM = pl.BlockSpec(memory_space=pltpu.VMEM)
SMEM = pl.BlockSpec(memory_space=pltpu.SMEM)
IMAGE = pltpu.VMEM((2 * ROWS, WIDTH), jnp.float32)
PHASE_ROWS = ROWS + QROWS
PHASES = ((2, 2, PHASE_ROWS, TILE), (2, TILES, 2, PHASE_ROWS, 128))
MATRIX = pltpu.VMEM((TAPS * TILE, TILE), jnp.bfloat16)


def exchange(value, distance):
    count = lax.axis_size("grp")
    return lax.ppermute(value, "grp", [(i, i ^ distance) for i in range(count)])


def split(value):
    high = value.astype(jnp.bfloat16)
    low = (value - high.astype(jnp.float32)).astype(jnp.bfloat16)
    return high, low


def fetch(sems, pairs):
    copies = [pltpu.make_async_copy(a, b, sems.at[i]) for i, (a, b) in enumerate(pairs)]
    for copy in copies:
        copy.start()
    return copies


def range_products(high, low, t_high, t_low, full, count):
    rows = count * 2 * ROWS
    dot = functools.partial(jnp.dot, preferred_element_type=jnp.float32)
    for index in range(5):
        first = index - 1
        taps = [t for t in range(TAPS) if 0 <= first + t < TILES]
        k0, k1 = taps[0] * TILE, (taps[-1] + 1) * TILE
        a0, a1 = k0 + first * TILE, k1 + first * TILE
        a_high = high[:count, :, a0:a1].reshape(rows, a1 - a0)
        a_low = low[:count, :, a0:a1].reshape(rows, a1 - a0)
        summed = dot(a_high, t_high[k0:k1, :]) + (
            dot(a_high, t_low[k0:k1, :]) + dot(a_low, t_high[k0:k1, :])
        )
        full[:count, :, index * TILE : (index + 1) * TILE] = summed.reshape(count, 2 * ROWS, TILE)
    full[:count, :, 5 * TILE :] = jnp.zeros((count, 2 * ROWS, TILE), jnp.float32)


def shifted(tiles):
    rows = tiles.shape[0]
    return [
        (tiles if k == 1 else pltpu.roll(tiles, (1 - k) % rows, 0))[8 : rows - 8] for k in range(4)
    ]


def unit(phases, e, row, count, lane):
    within, across = phases
    at = pl.ds(pl.multiple_of(lane % TILE, 128), LANES)
    n = lane // TILE
    c, s = (within[i, e, row : row + count, at] for i in range(2))
    cn, sn = (
        jnp.concatenate([across[i, n, e, row : row + count, :]] * (LANES // 128), 1)
        for i in range(2)
    )
    return c * cn - s * sn, s * cn + c * sn


def merge(section, block, lane, fulls, children, halves, offsets, w_ref, phases):
    r0, r1 = SPANS[block]
    out = [[None, None], [None, None]]
    for full, e in zip(fulls, children):

        def rows_at(offset, row, count):
            start = pl.multiple_of(offset * TILE + lane, 128)
            return full[row : row + count, pl.ds(start, LANES)]

        parts = []
        for base in (0, ROWS):
            if block == 0:
                o = offsets[section, e, 0]
                tiles = [rows_at(o, base + 32, 8), rows_at(o, base, 24)]
            elif block == 1:
                tiles = [rows_at(offsets[section, e, 1], base + 8, 32)]
            else:
                after, before = offsets[section, e, 2], offsets[section, e, 3]
                row = lax.broadcasted_iota(jnp.int32, (EDGE, LANES), 0)
                middle = jnp.where(
                    row < 4, rows_at(after, base + 32, 8), rows_at(before, base + 32, 8)
                )
                tiles = [rows_at(after, base + 24, 8), middle, rows_at(before, base, 8)]
            parts.append(shifted(jnp.concatenate(tiles, 0) if len(tiles) > 1 else tiles[0]))
        cosine, sine = unit(phases, e, section * ROWS + r0, r1 - r0, lane)
        for i, h in enumerate(halves):
            w = [w_ref[section, h, e, k] for k in range(4)]
            real, imag = (
                (w[0] * part[0] + w[1] * part[1]) + (w[2] * part[2] + w[3] * part[3])
                for part in parts
            )
            new = (real * cosine - imag * sine, real * sine + imag * cosine)
            out[i] = [n if o is None else o + n for o, n in zip(out[i], new)]
    return out


def first_merges(fulls, children, halves, where, offsets, w_ref, phases, high, low):
    @pl.loop(0, WIDTH, step=LANES)
    def _(lane):
        at = pl.ds(pl.multiple_of(lane, 128), LANES)
        blocks = [
            merge(0, b, lane, fulls, children, halves, offsets, w_ref, phases)
            for b in range(3)
        ]
        row = lax.broadcasted_iota(jnp.int32, (EDGE, LANES), 0)
        keep = jnp.where(row < 4, where[3], where[2]) > 0
        for i in range(2):
            merged = jnp.concatenate(
                [
                    jnp.where(keep, blocks[b][i][comp], 0.0) if b == 2 else blocks[b][i][comp]
                    for comp in range(2)
                    for b in range(3)
                ],
                0,
            )
            high[i, :, at], low[i, :, at] = split(merged)


def second_merges(fulls, children, halves, offsets, w_ref, phases, outs):
    @pl.loop(0, WIDTH, step=LANES)
    def _(lane):
        at = pl.ds(pl.multiple_of(lane, 128), LANES)
        for b in range(2):
            r0, r1 = SPANS[b]
            merged = merge(1, b, lane, fulls, children, halves, offsets, w_ref, phases)
            for i in range(2):
                for comp in range(2):
                    outs[i][comp, r0:r1, at] = merged[i][comp]


def ends_kernel(rates_in, offs_in, image, tail, head, edges, rates, offs, sems):
    copies = fetch(
        sems,
        [
            (image.at[:, 0:8], edges.at[0]), (image.at[:, 120:128], edges.at[1]),
            (rates_in.at[0], rates), (offs_in.at[0], offs),
        ],
    )
    lane = lax.broadcasted_iota(jnp.int32, (1, WIDTH), 1)

    def line(*values):
        out = jnp.zeros((1, WIDTH), jnp.float32)
        for i, value in enumerate(values):
            out = jnp.where(lane == i, value, out)
        return out

    for copy in copies:
        copy.wait()

    def offset(e, block):
        return offs[e, block].astype(jnp.float32)

    tail[0:2] = edges[1, 0, 6:8]
    tail[2:4] = edges[1, 1, 6:8]
    tail[4:5] = line(rates[0, 127], rates[1, 127], offset(0, 7), offset(1, 7))
    tail[5:8] = jnp.zeros((3, WIDTH), jnp.float32)
    head[0:4] = edges[0, 0, 0:4]
    head[4:8] = edges[0, 1, 0:4]
    head[8:9] = line(rates[0, 0], rates[0, 1], rates[1, 0], rates[1, 1], offset(0, 0), offset(1, 0))
    head[9:16] = jnp.zeros((7, WIDTH), jnp.float32)


def quarters_kernel(distances, where, image, before, after, *refs):
    count = len(distances)
    outs, (stages, rows, sems, out_sems) = refs[:count], refs[-4:]
    copies = []
    for n, d in enumerate(distances):
        q = where[4] ^ d
        trail = pl.multiple_of(jnp.minimum(q * QROWS + QROWS, 120), 8)
        lead = pl.multiple_of(jnp.maximum(q * QROWS - 8, 0), 8)
        part = pl.ds(pl.multiple_of(q * QROWS, QROWS), QROWS)
        copies.append((image.at[:, pl.ds(trail, 8)], rows.at[n, 0]))
        copies.append((image.at[:, pl.ds(lead, 8)], rows.at[n, 1]))
        copies.append((image.at[:, part], stages.at[n, :, :QROWS]))
    copies = fetch(sems, copies)
    writes = []
    for n, d in enumerate(distances):
        q = where[4] ^ d
        copies[3 * n].wait()
        copies[3 * n + 1].wait()
        for comp in range(2):
            stages[n, comp, QROWS : QROWS + 4] = jnp.where(
                q == 3, after[4 * comp : 4 * comp + 4], rows[n, 0, comp, 0:4]
            )
            stages[n, comp, QROWS + 4 : QROWS + 6] = jnp.zeros((2, WIDTH), jnp.float32)
            stages[n, comp, QROWS + 6 :] = jnp.where(
                q == 0, before[2 * comp : 2 * comp + 2], rows[n, 1, comp, 6:8]
            )
        copies[3 * n + 2].wait()
        writes += fetch(out_sems.at[n : n + 1], [(stages.at[n], outs[n])])
    for copy in writes:
        copy.wait()


def split_tiles(values, high, low):
    @pl.loop(0, TAPS * TILE, step=64)
    def _(row):
        at = pl.ds(pl.multiple_of(row, 64), 64)
        high[at], low[at] = split(values[at])


def own_kernel(tiles, q0, full1_out, t_high, t_low, high, low, full, t1, t2, th, tl, sems, out_sems):
    copies = fetch(sems, [(tiles.at[0], t1), (tiles.at[1], t2)])
    high[0], low[0] = split(q0[...].reshape(2 * ROWS, WIDTH))
    copies[0].wait()
    split_tiles(t1, th.at[0], tl.at[0])
    outs = fetch(out_sems, [(th.at[0], t_high.at[0]), (tl.at[0], t_low.at[0])])
    range_products(high, low, th.at[0], tl.at[0], full, 1)
    outs += fetch(out_sems.at[2:3], [(full.at[0], full1_out)])
    copies[1].wait()
    split_tiles(t2, th.at[1], tl.at[1])
    outs += fetch(out_sems.at[3:5], [(th.at[1], t_high.at[1]), (tl.at[1], t_low.at[1])])
    for copy in outs:
        copy.wait()


def early_kernel(
    where, offsets, w_ref, full1_in, m1, m3, t_high, t_low, within, across,
    full1_out, full2_out,
    image1, image3, high, low, full, full2, ph1, ph2, th1, tl1, th2, tl2, sems, out_sems,
):
    copies = fetch(
        sems,
        [
            (m1, image1), (m3, image3), (t_high.at[0], th1), (t_low.at[0], tl1),
            (full1_in, full.at[2]), (within, ph1), (across, ph2),
            (t_high.at[1], th2), (t_low.at[1], tl2),
        ],
    )
    phases = (ph1, ph2)
    bit = where[0]
    for slot, image in enumerate((image1, image3)):
        copies[slot].wait()
        high[slot], low[slot] = split(image[...].reshape(2 * ROWS, WIDTH))
    copies[2].wait()
    copies[3].wait()
    range_products(high, low, th1, tl1, full, 2)
    outs = fetch(out_sems, [(full.at[1], full1_out)])
    for copy in copies[4:7]:
        copy.wait()
    first_merges(
        (full.at[2], full.at[0]), (bit, 1 - bit), (bit, 1 - bit),
        where, offsets, w_ref, phases, high, low,
    )
    copies[7].wait()
    copies[8].wait()
    range_products(high, low, th2, tl2, full2, 2)
    outs += fetch(out_sems.at[1:2], [(full2, full2_out)])
    for copy in outs:
        copy.wait()


def middle_kernel(
    where, offsets, w_ref, image, full1_in, full2_in, t_high, t_low, within, across,
    d2, result, full2_out,
    rows, fulls, ph1, ph2, high, low, full2, d0, th1, tl1, th2, tl2, sems, out_sems,
):
    copies = fetch(
        sems,
        [
            (image, rows), (t_high.at[0], th1), (t_low.at[0], tl1), (full1_in, fulls.at[1]),
            (within, ph1), (across, ph2), (t_high.at[1], th2), (t_low.at[1], tl2),
            (full2_in.at[0], fulls.at[2]),
        ],
    )
    phases = (ph1, ph2)
    bit, bit2 = where[0], where[1]
    copies[0].wait()
    high[0], low[0] = split(rows[...].reshape(2 * ROWS, WIDTH))
    copies[1].wait()
    copies[2].wait()
    range_products(high, low, th1, tl1, fulls, 1)
    for copy in copies[3:6]:
        copy.wait()
    first_merges(
        (fulls.at[0], fulls.at[1]), (bit, 1 - bit), (bit, 1 - bit),
        where, offsets, w_ref, phases, high, low,
    )
    copies[6].wait()
    copies[7].wait()
    range_products(high, low, th2, tl2, full2, 2)
    out = pltpu.make_async_copy(full2.at[1], full2_out, out_sems.at[0])
    out.start()
    copies[8].wait()
    second_merges(
        (fulls.at[2], full2.at[0]), (bit2, 1 - bit2), (bit2, 1 - bit2),
        offsets, w_ref, phases, (d0, d2),
    )
    at = pl.ds(pl.multiple_of(where[4] * QROWS, QROWS), QROWS)
    kept = pltpu.make_async_copy(d0, result.at[:, at], out_sems.at[1])
    kept.start()
    out.wait()
    kept.wait()


def late_kernel(
    where, offsets, w_ref, full2_in, full_b, within, across, d1, d3, fa, fb, ph1, ph2, sems
):
    bit2 = where[1]
    copies = fetch(
        sems, [(full2_in.at[1], fa), (full_b, fb), (within, ph1), (across, ph2)]
    )
    for copy in copies:
        copy.wait()
    second_merges(
        (fa, fb), (bit2, 1 - bit2), (bit2, 1 - bit2), offsets, w_ref, (ph1, ph2), (d1, d3)
    )


def place_kernel(distances, where, *refs):
    pieces, out, sems = refs[: len(distances)], refs[-2], refs[-1]
    copies = []
    for i, d in enumerate(distances):
        at = pl.ds(pl.multiple_of((where[4] ^ d) * QROWS, QROWS), QROWS)
        copies.append(pltpu.make_async_copy(pieces[i], out.at[:, at], sems.at[i]))
        copies[-1].start()
    for copy in copies:
        copy.wait()


def call(kernel, name, outs, in_specs, out_specs, scratch, flops, moved, aliases=None):
    return pl.pallas_call(
        kernel,
        out_shape=[jax.ShapeDtypeStruct(shape, kind) for shape, kind in outs],
        in_specs=in_specs,
        out_specs=out_specs,
        scratch_shapes=scratch,
        input_output_aliases=aliases or {},
        compiler_params=pltpu.CompilerParams(vmem_limit_bytes=52 * 2**20),
        cost_estimate=pl.CostEstimate(flops=flops, bytes_accessed=moved, transcendentals=0),
        name=name,
    )


def halves_scratch(count):
    return [pltpu.VMEM((count, 2 * ROWS, WIDTH), jnp.bfloat16)] * 2


def full_scratch(count):
    return pltpu.VMEM((count, 2 * ROWS, FULL), jnp.float32)


def per_device(subimages, beam_weights, range_tiles, tile_offsets, phase_rates):
    f32, bf16 = jnp.float32, jnp.bfloat16
    dma = pltpu.SemaphoreType.DMA
    mine = lax.axis_index("grp") & 3
    beam = lax.axis_index("beam")
    beams = lax.axis_size("beam")
    image = subimages.reshape(2, RING * QROWS, WIDTH)
    first = jnp.logical_and(beam == 0, mine == 0)
    last = jnp.logical_and(beam == beams - 1, mine == 3)
    where = jnp.stack(
        [mine & 1, mine >> 1, 1 - first.astype(jnp.int32), 1 - last.astype(jnp.int32), mine]
    ).astype(jnp.int32)
    piece_shape = ((2, QROWS, WIDTH), f32)
    quarter_shape = ((2, ROWS, WIDTH), f32)
    tail, head = call(
        ends_kernel, "ends", [((8, WIDTH), f32), ((16, WIDTH), f32)], [HBM] * 3, [VMEM] * 2,
        [pltpu.VMEM((2, 2, 8, WIDTH), f32), pltpu.SMEM((2, 4 * QROWS), f32)]
        + [pltpu.SMEM((2, 8), jnp.int32), dma((4,))],
        10**6, 2**20,
    )(phase_rates, tile_offsets, image)
    before = lax.ppermute(tail, "beam", [(i, i + 1) for i in range(beams - 1)])
    after = lax.ppermute(head, "beam", [(i + 1, i) for i in range(beams - 1)])

    def quarters(*distances):
        count = len(distances)
        return call(
            functools.partial(quarters_kernel, distances), "quarters", [quarter_shape] * count,
            [SMEM, HBM, VMEM, VMEM], [HBM] * count,
            [pltpu.VMEM((count, 2, ROWS, WIDTH), f32), pltpu.VMEM((count, 2, 2, 8, WIDTH), f32)]
            + [dma((3 * count,)), dma((count,))],
            10**6, 3 * 2**20,
        )(where, image, before, after)

    q1, q3 = quarters(1, 3)
    m1 = exchange(q1, 1)
    m3 = exchange(q3, 3)
    q2, q0 = quarters(2, 0)
    q2, m1 = lax.optimization_barrier((q2, m1))
    m2 = exchange(q2, 2)

    before_values, after_values = before[4, :4].reshape(2, 2), after[8, :6]
    line = jnp.concatenate([before_values[0][:, None], phase_rates[0], after_values[:4].reshape(2, 2)], 1)
    line = lax.dynamic_slice_in_dim(line, mine * QROWS, QROWS + 3, 1)
    rates_b = lax.dynamic_slice_in_dim(phase_rates[1], mine * QROWS, QROWS, 1)
    rates = jnp.concatenate([line[:, 1:], jnp.zeros((2, 5), f32), line[:, :1], rates_b], 1)
    offs = tile_offsets[0].astype(f32)
    line = jnp.concatenate([before_values[1][:, None], offs, after_values[4:][:, None]], 1)
    line = lax.dynamic_slice_in_dim(line, mine * 2, 4, 1).astype(jnp.int32)
    offs_a = jnp.stack([line[:, 1], line[:, 2], line[:, 3], line[:, 0]], 1)
    offs_b = jnp.pad(lax.dynamic_slice_in_dim(tile_offsets[1], mine * 2, 2, 1), ((0, 0), (0, 2)))
    offsets = jnp.clip(jnp.stack([offs_a, offs_b]), 0, 2)
    angles = rates[:, :, None] * (jnp.arange(TILE, dtype=f32) / TILE)
    within = jnp.stack([jnp.cos(angles), jnp.sin(angles)])
    angles = jnp.arange(TILES, dtype=f32)[:, None, None, None] * rates[:, :, None]
    angles = jnp.broadcast_to(angles, (TILES, 2, PHASE_ROWS, 128))
    across = jnp.stack([jnp.cos(angles), jnp.sin(angles)])

    scalars = (where, offsets, beam_weights)
    full_shape = (2 * ROWS, FULL)
    tables = [pltpu.VMEM(shape, f32) for shape in PHASES]
    matrix_shape = ((2, TAPS * TILE, TILE), bf16)
    full1_0, t_high, t_low = call(
        own_kernel, "own", [(full_shape, f32), matrix_shape, matrix_shape], [HBM, VMEM], [HBM] * 3,
        halves_scratch(1) + [full_scratch(1)] + [pltpu.VMEM((TAPS * TILE, TILE), f32)] * 2
        + [pltpu.VMEM(*matrix_shape)] * 2 + [dma((2,)), dma((5,))],
        5 * 10**9, 14 * 2**20,
    )(range_tiles.reshape(2, TAPS * TILE, TILE), q0)
    full1, full2 = call(
        early_kernel, "early", [(full_shape, f32), ((2, *full_shape), f32)],
        [SMEM] * 3 + [HBM] * 7, [HBM] * 2,
        [pltpu.VMEM(*quarter_shape)] * 2 + halves_scratch(2) + [full_scratch(3), full_scratch(2)]
        + tables + [MATRIX] * 4 + [dma((9,)), dma((2,))],
        10 * 10**9, 16 * 2**20,
    )(*scalars, full1_0, m1, m3, t_high, t_low, within, across)
    d2, result, full2_3 = call(
        middle_kernel, "middle",
        [piece_shape, ((2, RING * QROWS, WIDTH), f32), (full_shape, f32)],
        [SMEM] * 3 + [HBM] * 7, [VMEM] + [HBM] * 2,
        [pltpu.VMEM((2, ROWS, WIDTH), f32), full_scratch(3), *tables]
        + halves_scratch(2) + [full_scratch(2), pltpu.VMEM((2, QROWS, WIDTH), f32)]
        + [MATRIX] * 4 + [dma((9,)), dma((2,))],
        9 * 10**9, 10 * 2**20,
    )(*scalars, m2, full1, full2, t_high, t_low, within, across)
    r2 = exchange(d2, 2)
    d1, d3 = call(
        late_kernel, "late", [piece_shape] * 2, [SMEM] * 3 + [HBM] * 4, [VMEM] * 2,
        [pltpu.VMEM(full_shape, f32)] * 2 + tables + [dma((4,))],
        4 * 10**9, 4 * 2**20,
    )(*scalars, full2, full2_3, within, across)
    r1 = exchange(d1, 1)
    r3 = exchange(d3, 3)

    for distances, pieces, flops in (((2,), (r2,), 10**11), ((1, 3), (r1, r3), 10**5)):
        (result,) = call(
            functools.partial(place_kernel, distances), "place", [(result.shape, f32)],
            [SMEM] + [HBM] * (len(pieces) + 1), [HBM], [dma((len(pieces),))],
            flops, 2**21, {1 + len(pieces): 0},
        )(where, *pieces, result)
    return result[:, None]


def solution(mesh):
    return jax.shard_map(
        per_device,
        mesh=mesh,
        in_specs=(
            P(None, "grp", "beam", None),
            P(),
            P(),
            P(None, None, "beam"),
            P(None, None, "beam"),
        ),
        out_specs=P(None, "grp", "beam", None),
        check_vma=False,
    )
```

```python
import functools

import jax
import jax.numpy as jnp
from jax import lax
from jax.experimental import pallas as pl
from jax.experimental.pallas import tpu as pltpu
from jax.sharding import PartitionSpec as P

TILE = 512
TAPS = 3
BLK = 16
RING = 4
QROWS = 32
EDGE = 8
ROWS = QROWS + EDGE
WIDTH = 2048
TILES = WIDTH // TILE
FULL = WIDTH + 2 * TILE
LANES = 512
SPANS = ((0, 16), (16, 32), (32, 40))
HBM = pl.BlockSpec(memory_space=pltpu.HBM)
VMEM = pl.BlockSpec(memory_space=pltpu.VMEM)
SMEM = pl.BlockSpec(memory_space=pltpu.SMEM)
IMAGE = pltpu.VMEM((2 * ROWS, WIDTH), jnp.float32)
PHASE_ROWS = ROWS + QROWS
PHASES = ((2, 2, PHASE_ROWS, TILE), (2, TILES, 2, PHASE_ROWS, 128))
MATRIX = pltpu.VMEM((TAPS * TILE, TILE), jnp.bfloat16)


def exchange(value, distance):
    count = lax.axis_size("grp")
    return lax.ppermute(value, "grp", [(i, i ^ distance) for i in range(count)])


def split(value):
    high = value.astype(jnp.bfloat16)
    low = (value - high.astype(jnp.float32)).astype(jnp.bfloat16)
    return high, low


def fetch(sems, pairs):
    copies = [pltpu.make_async_copy(a, b, sems.at[i]) for i, (a, b) in enumerate(pairs)]
    for copy in copies:
        copy.start()
    return copies


def range_products(high, low, t_high, t_low, full, count):
    rows = count * 2 * ROWS
    dot = functools.partial(jnp.dot, preferred_element_type=jnp.float32)
    full[:count, :, 5 * TILE :] = jnp.zeros((count, 2 * ROWS, TILE), jnp.float32)
    if count == 1:
        parts = [
            [part[0, :, m * TILE : (m + 1) * TILE] for m in range(TILES)] for part in (high, low)
        ]
        for t in range(TAPS):
            uses = [m for m in range(TILES) if m - t >= -1]
            n = len(uses) * rows
            a_high, a_low = ([part[m] for m in uses] for part in parts)
            at = slice(t * TILE, (t + 1) * TILE)
            both = dot(jnp.concatenate(a_high + a_low, 0), t_high[at, :])
            summed = both[:n] + both[n:] + dot(jnp.concatenate(a_high, 0), t_low[at, :])
            for i, m in enumerate(uses):
                to = slice((m - t + 1) * TILE, (m - t + 2) * TILE)
                value = summed[i * rows : (i + 1) * rows]
                full[0, :, to] = value if t == 0 or m == 0 else full[0, :, to] + value
        return
    for index in range(5):
        first = index - 1
        taps = [t for t in range(TAPS) if 0 <= first + t < TILES]
        k0, k1 = taps[0] * TILE, (taps[-1] + 1) * TILE
        a0, a1 = k0 + first * TILE, k1 + first * TILE
        a_high = high[:count, :, a0:a1].reshape(rows, a1 - a0)
        a_low = low[:count, :, a0:a1].reshape(rows, a1 - a0)
        summed = dot(a_high, t_high[k0:k1, :]) + (
            dot(a_high, t_low[k0:k1, :]) + dot(a_low, t_high[k0:k1, :])
        )
        full[:count, :, index * TILE : (index + 1) * TILE] = summed.reshape(count, 2 * ROWS, TILE)


def shifted(tiles):
    rows = tiles.shape[0]
    return [
        (tiles if k == 1 else pltpu.roll(tiles, (1 - k) % rows, 0))[8 : rows - 8] for k in range(4)
    ]


def unit(phases, e, row, count, lane):
    within, across = phases
    at = pl.ds(pl.multiple_of(lane % TILE, 128), LANES)
    n = lane // TILE
    c, s = (within[i, e, row : row + count, at] for i in range(2))
    cn, sn = (
        jnp.concatenate([across[i, n, e, row : row + count, :]] * (LANES // 128), 1)
        for i in range(2)
    )
    return c * cn - s * sn, s * cn + c * sn


def merge(section, block, lane, fulls, children, halves, offsets, w_ref, phases):
    r0, r1 = SPANS[block]
    out = [[None, None] for _ in halves]
    for full, e in zip(fulls, children):

        def rows_at(offset, row, count):
            start = pl.multiple_of(offset * TILE + lane, 128)
            return full[row : row + count, pl.ds(start, LANES)]

        parts = []
        for base in (0, ROWS):
            if block == 0:
                o = offsets[section, e, 0]
                tiles = [rows_at(o, base + 32, 8), rows_at(o, base, 24)]
            elif block == 1:
                tiles = [rows_at(offsets[section, e, 1], base + 8, 32)]
            else:
                after, before = offsets[section, e, 2], offsets[section, e, 3]
                row = lax.broadcasted_iota(jnp.int32, (EDGE, LANES), 0)
                middle = jnp.where(
                    row < 4, rows_at(after, base + 32, 8), rows_at(before, base + 32, 8)
                )
                tiles = [rows_at(after, base + 24, 8), middle, rows_at(before, base, 8)]
            parts.append(shifted(jnp.concatenate(tiles, 0) if len(tiles) > 1 else tiles[0]))
        cosine, sine = unit(phases, e, section * ROWS + r0, r1 - r0, lane)
        for i, h in enumerate(halves):
            w = [w_ref[section, h, e, k] for k in range(4)]
            real, imag = (
                (w[0] * part[0] + w[1] * part[1]) + (w[2] * part[2] + w[3] * part[3])
                for part in parts
            )
            new = (real * cosine - imag * sine, real * sine + imag * cosine)
            out[i] = [n if o is None else o + n for o, n in zip(out[i], new)]
    return out


def first_merges(fulls, children, halves, where, offsets, w_ref, phases, high, low):
    @pl.loop(0, WIDTH, step=LANES)
    def _(lane):
        at = pl.ds(pl.multiple_of(lane, 128), LANES)
        blocks = [
            merge(0, b, lane, fulls, children, halves, offsets, w_ref, phases)
            for b in range(3)
        ]
        row = lax.broadcasted_iota(jnp.int32, (EDGE, LANES), 0)
        keep = jnp.where(row < 4, where[3], where[2]) > 0
        for i in range(len(halves)):
            merged = jnp.concatenate(
                [
                    jnp.where(keep, blocks[b][i][comp], 0.0) if b == 2 else blocks[b][i][comp]
                    for comp in range(2)
                    for b in range(3)
                ],
                0,
            )
            high[i, :, at], low[i, :, at] = split(merged)


def second_merges(fulls, children, halves, offsets, w_ref, phases, outs):
    @pl.loop(0, WIDTH, step=LANES)
    def _(lane):
        at = pl.ds(pl.multiple_of(lane, 128), LANES)
        for b in range(2):
            r0, r1 = SPANS[b]
            merged = merge(1, b, lane, fulls, children, halves, offsets, w_ref, phases)
            for i in range(len(halves)):
                for comp in range(2):
                    outs[i][comp, r0:r1, at] = merged[i][comp]


def pack_kernel(
    rates_in, offs_in, where, image, q1, q3, tail, head, edges, rates, offs, sems
):
    copies = fetch(
        sems,
        [
            (image.at[:, 0:8], edges.at[0]), (image.at[:, 120:128], edges.at[1]),
            (rates_in.at[0], rates), (offs_in.at[0], offs),
        ]
        + [
            (image.at[:, pl.ds(pl.multiple_of((where[4] ^ d) * QROWS, QROWS), QROWS)], out)
            for d, out in ((1, q1), (3, q3))
        ],
    )
    lane = lax.broadcasted_iota(jnp.int32, (1, WIDTH), 1)

    def line(*values):
        out = jnp.zeros((1, WIDTH), jnp.float32)
        for i, value in enumerate(values):
            out = jnp.where(lane == i, value, out)
        return out

    for copy in copies[:4]:
        copy.wait()

    def offset(e, block):
        return offs[e, block].astype(jnp.float32)

    tail[0:2] = edges[1, 0, 6:8]
    tail[2:4] = edges[1, 1, 6:8]
    tail[4:5] = line(rates[0, 127], rates[1, 127], offset(0, 7), offset(1, 7))
    tail[5:8] = jnp.zeros((3, WIDTH), jnp.float32)
    head[0:4] = edges[0, 0, 0:4]
    head[4:8] = edges[0, 1, 0:4]
    head[8:9] = line(rates[0, 0], rates[0, 1], rates[1, 0], rates[1, 1], offset(0, 0), offset(1, 0))
    head[9:16] = jnp.zeros((7, WIDTH), jnp.float32)
    for copy in copies[4:]:
        copy.wait()


def rims_kernel(where, image, before, after, e0, p1, p3, stage, rows, sems):
    copies = []
    for d in range(RING):
        q = where[4] ^ d
        trail = pl.multiple_of(jnp.minimum(q * QROWS + QROWS, 120), 8)
        lead = pl.multiple_of(jnp.maximum(q * QROWS - 8, 0), 8)
        copies.append((image.at[:, pl.ds(trail, 8)], rows.at[d, 0]))
        copies.append((image.at[:, pl.ds(lead, 8)], rows.at[d, 1]))
    part = pl.ds(pl.multiple_of((where[4] ^ 2) * QROWS, QROWS), QROWS)
    copies = fetch(sems, copies + [(image.at[:, part], stage.at[:, :QROWS])])
    for copy in copies:
        copy.wait()
    for d, (out, r) in enumerate(((e0, 0), (p1, 0), (stage, QROWS), (p3, 0))):
        q = where[4] ^ d
        for comp in range(2):
            out[comp, r : r + 4] = jnp.where(
                q == 3, after[4 * comp : 4 * comp + 4], rows[d, 0, comp, 0:4]
            )
            out[comp, r + 4 : r + 6] = jnp.zeros((2, WIDTH), jnp.float32)
            out[comp, r + 6 : r + 8] = jnp.where(
                q == 0, before[2 * comp : 2 * comp + 2], rows[d, 1, comp, 6:8]
            )


def split_tiles(values, high, low):
    @pl.loop(0, TAPS * TILE, step=64)
    def _(row):
        at = pl.ds(pl.multiple_of(row, 64), 64)
        high[at], low[at] = split(values[at])


def fill(image, rim, high, low):
    rows = jnp.concatenate([image[...], rim[...]], 1)
    high[...], low[...] = split(rows.reshape(2 * ROWS, WIDTH))


def own_kernel(where, tiles, image, e0, full1_0, th, tl, main, high, low, t1, sems):
    part = pl.ds(pl.multiple_of(where[4] * QROWS, QROWS), QROWS)
    copies = fetch(sems, [(tiles.at[0], t1), (image.at[:, part], main)])
    copies[1].wait()
    fill(main, e0, high.at[0], low.at[0])
    copies[0].wait()
    split_tiles(t1, th, tl)
    range_products(high, low, th, tl, full1_0, 1)


def early_kernel(
    where, offsets, w_ref, full1_0, m1, e1, m3, e3, th1, tl1, tiles, within, across,
    full1, full2, th2, tl2,
    high, low, t2, sems,
):
    copies = fetch(sems, [(tiles.at[1], t2)])
    bit = where[0]
    fill(m1, e1, high.at[0], low.at[0])
    fill(m3, e3, high.at[1], low.at[1])
    range_products(high, low, th1, tl1, full1, 2)
    first_merges(
        (full1_0.at[0], full1.at[0]), (bit, 1 - bit), (bit, 1 - bit),
        where, offsets, w_ref, (within, across), high, low,
    )
    copies[0].wait()
    split_tiles(t2, th2, tl2)
    range_products(high, low, th2, tl2, full2, 2)


def middle_kernel(
    where, offsets, w_ref, m2, full1, full2, th1, tl1, th2, tl2, within, across,
    d2, full1_2, full2_2,
    high, low,
):
    phases = (within, across)
    bit, bit2 = where[0], where[1]
    high[0], low[0] = split(m2[...].reshape(2 * ROWS, WIDTH))
    range_products(high, low, th1, tl1, full1_2, 1)
    first_merges(
        (full1_2.at[0], full1.at[1]), (bit, 1 - bit), (bit,),
        where, offsets, w_ref, phases, high, low,
    )
    range_products(high, low, th2, tl2, full2_2, 1)
    second_merges(
        (full2.at[0], full2_2.at[0]), (bit2, 1 - bit2), (1 - bit2,),
        offsets, w_ref, phases, (d2,),
    )


def late_kernel(
    where, offsets, w_ref, full1_2, full1, full2, th2, tl2, within, across,
    d1, d3,
    high, low, full2_3,
):
    phases = (within, across)
    bit, bit2 = where[0], where[1]
    first_merges(
        (full1_2.at[0], full1.at[1]), (bit, 1 - bit), (1 - bit,),
        where, offsets, w_ref, phases, high, low,
    )
    range_products(high, low, th2, tl2, full2_3, 1)
    second_merges(
        (full2.at[1], full2_3.at[0]), (bit2, 1 - bit2), (bit2, 1 - bit2),
        offsets, w_ref, phases, (d1, d3),
    )


def rest_kernel(where, offsets, w_ref, full2, full2_2, within, across, result, d0, sems):
    bit2 = where[1]
    second_merges(
        (full2.at[0], full2_2.at[0]), (bit2, 1 - bit2), (bit2,),
        offsets, w_ref, (within, across), (d0,),
    )
    at = pl.ds(pl.multiple_of(where[4] * QROWS, QROWS), QROWS)
    for copy in fetch(sems, [(d0, result.at[:, at])]):
        copy.wait()


def place_kernel(distances, where, *refs):
    pieces, (out, stages, sems, out_sems) = refs[: len(distances)], refs[-4:]
    reads, writes = [], []
    for i, d in enumerate(distances):
        for n in range(2):
            at = pl.ds(pl.multiple_of((where[4] ^ d) * QROWS + 16 * n, 16), 16)
            half = stages.at[i, :, 16 * n : 16 * n + 16]
            reads.append((pieces[i].at[:, 16 * n : 16 * n + 16], half))
            writes.append((half, out.at[:, at]))
    reads = fetch(sems, reads)
    copies = []
    for i, pair in enumerate(writes):
        reads[i].wait()
        copies += fetch(out_sems.at[i : i + 1], [pair])
    for copy in copies:
        copy.wait()


def call(kernel, name, outs, in_specs, out_specs, scratch, flops, moved, aliases=None, vmem=8):
    return pl.pallas_call(
        kernel,
        out_shape=[jax.ShapeDtypeStruct(shape, kind) for shape, kind in outs],
        in_specs=in_specs,
        out_specs=out_specs,
        scratch_shapes=scratch,
        input_output_aliases=aliases or {},
        compiler_params=pltpu.CompilerParams(vmem_limit_bytes=vmem * 2**20),
        cost_estimate=pl.CostEstimate(flops=flops, bytes_accessed=moved, transcendentals=0),
        name=name,
    )


def halves_scratch(count):
    return [pltpu.VMEM((count, 2 * ROWS, WIDTH), jnp.bfloat16)] * 2


def full_scratch(count):
    return pltpu.VMEM((count, 2 * ROWS, FULL), jnp.float32)


def per_device(subimages, beam_weights, range_tiles, tile_offsets, phase_rates):
    f32, bf16 = jnp.float32, jnp.bfloat16
    dma = pltpu.SemaphoreType.DMA
    mine = lax.axis_index("grp") & 3
    beam = lax.axis_index("beam")
    beams = lax.axis_size("beam")
    image = subimages.reshape(2, RING * QROWS, WIDTH)
    first = jnp.logical_and(beam == 0, mine == 0)
    last = jnp.logical_and(beam == beams - 1, mine == 3)
    where = jnp.stack(
        [mine & 1, mine >> 1, 1 - first.astype(jnp.int32), 1 - last.astype(jnp.int32), mine]
    ).astype(jnp.int32)
    piece_shape = ((2, QROWS, WIDTH), f32)
    quarter_shape = ((2, ROWS, WIDTH), f32)
    q1, q3, tail, head = call(
        pack_kernel, "pack", [piece_shape, piece_shape, ((8, WIDTH), f32), ((16, WIDTH), f32)],
        [HBM] * 2 + [SMEM] + [HBM], [VMEM] * 4,
        [pltpu.VMEM((2, 2, 8, WIDTH), f32), pltpu.SMEM((2, 4 * QROWS), f32)]
        + [pltpu.SMEM((2, 8), jnp.int32), dma((6,))],
        10**6, 2**20, vmem=62,
    )(phase_rates, tile_offsets, where, image)
    m1 = exchange(q1, 1)
    m3 = exchange(q3, 3)
    before = lax.ppermute(tail, "beam", [(i, i + 1) for i in range(beams - 1)])
    after = lax.ppermute(head, "beam", [(i + 1, i) for i in range(beams - 1)])
    rim_shape = ((2, EDGE, WIDTH), f32)
    e0, p1, p3, q2 = call(
        rims_kernel, "rims", [rim_shape] * 3 + [quarter_shape],
        [SMEM, HBM, VMEM, VMEM], [VMEM] * 4,
        [pltpu.VMEM((RING, 2, 2, 8, WIDTH), f32), dma((9,))],
        10**6, 3 * 2**20,
    )(where, image, before, after)
    e1 = exchange(p1, 1)
    e3 = exchange(p3, 3)
    q2, m1, e0 = lax.optimization_barrier((q2, m1, e0))
    m2 = exchange(q2, 2)

    before_values, after_values = before[4, :4].reshape(2, 2), after[8, :6]
    line = jnp.concatenate([before_values[0][:, None], phase_rates[0], after_values[:4].reshape(2, 2)], 1)
    line = lax.dynamic_slice_in_dim(line, mine * QROWS, QROWS + 3, 1)
    rates_b = lax.dynamic_slice_in_dim(phase_rates[1], mine * QROWS, QROWS, 1)
    rates = jnp.concatenate([line[:, 1:], jnp.zeros((2, 5), f32), line[:, :1], rates_b], 1)
    offs = tile_offsets[0].astype(f32)
    line = jnp.concatenate([before_values[1][:, None], offs, after_values[4:][:, None]], 1)
    line = lax.dynamic_slice_in_dim(line, mine * 2, 4, 1).astype(jnp.int32)
    offs_a = jnp.stack([line[:, 1], line[:, 2], line[:, 3], line[:, 0]], 1)
    offs_b = jnp.pad(lax.dynamic_slice_in_dim(tile_offsets[1], mine * 2, 2, 1), ((0, 0), (0, 2)))
    offsets = jnp.clip(jnp.stack([offs_a, offs_b]), 0, 2)
    angles = rates[:, :, None] * (jnp.arange(TILE, dtype=f32) / TILE)
    within = jnp.stack([jnp.cos(angles), jnp.sin(angles)])
    angles = jnp.arange(TILES, dtype=f32)[:, None, None, None] * rates[:, :, None]
    angles = jnp.broadcast_to(angles, (TILES, 2, PHASE_ROWS, 128))
    across = jnp.stack([jnp.cos(angles), jnp.sin(angles)])

    scalars = (where, offsets, beam_weights)
    full_shape = (2 * ROWS, FULL)
    one, two = ((1, *full_shape), f32), ((2, *full_shape), f32)
    matrix_shape = ((TAPS * TILE, TILE), bf16)
    matrices = range_tiles.reshape(2, TAPS * TILE, TILE)
    matrix_f32 = pltpu.VMEM((TAPS * TILE, TILE), f32)
    full1_0, t1h, t1l = call(
        own_kernel, "own", [one, matrix_shape, matrix_shape], [SMEM] + [HBM] * 2 + [VMEM],
        [VMEM] * 3, [pltpu.VMEM(*piece_shape)] + halves_scratch(1) + [matrix_f32, dma((2,))],
        30 * 10**9, 8 * 2**20, vmem=16,
    )(where, matrices, image, e0)
    full1, full2, t2h, t2l = call(
        early_kernel, "early", [two, two, matrix_shape, matrix_shape],
        [SMEM] * 3 + [VMEM] * 7 + [HBM] + [VMEM] * 2, [VMEM] * 4,
        halves_scratch(2) + [matrix_f32, dma((1,))],
        10**4, 10**4, vmem=28,
    )(*scalars, full1_0, m1, e1, m3, e3, t1h, t1l, matrices, within, across)
    d2, full1_2, full2_2 = call(
        middle_kernel, "middle", [piece_shape, one, one],
        [SMEM] * 3 + [VMEM] * 9, [VMEM] * 3, halves_scratch(1),
        9 * 10**9, 10 * 2**20, vmem=24,
    )(*scalars, m2, full1, full2, t1h, t1l, t2h, t2l, within, across)
    r2 = exchange(d2, 2)
    d1, d3 = call(
        late_kernel, "late", [piece_shape] * 2, [SMEM] * 3 + [VMEM] * 7, [VMEM] * 2,
        halves_scratch(1) + [full_scratch(1)],
        7 * 10**9, 4 * 2**20, vmem=20,
    )(*scalars, full1_2, full1, full2, t2h, t2l, within, across)
    r1 = exchange(d1, 1)
    r3 = exchange(d3, 3)
    (result,) = call(
        rest_kernel, "rest", [((2, RING * QROWS, WIDTH), f32)], [SMEM] * 3 + [VMEM] * 4, [HBM],
        [pltpu.VMEM(*piece_shape), dma((1,))],
        3 * 10**9, 3 * 2**20, vmem=12,
    )(*scalars, full2, full2_2, within, across)

    for distances, pieces, flops in (((2,), (r2,), 10**11), ((1, 3), (r1, r3), 10**5)):
        (result,) = call(
            functools.partial(place_kernel, distances), "place", [(result.shape, f32)],
            [SMEM] + [HBM] * (len(pieces) + 1), [HBM],
            [pltpu.VMEM((len(pieces), *piece_shape[0]), f32)] + [dma((2 * len(pieces),))] * 2,
            flops, 2**21, {1 + len(pieces): 0},
        )(where, *pieces, result)
    return result[:, None]


def solution(mesh):
    return jax.shard_map(
        per_device,
        mesh=mesh,
        in_specs=(
            P(None, "grp", "beam", None),
            P(),
            P(),
            P(None, None, "beam"),
            P(None, None, "beam"),
        ),
        out_specs=P(None, "grp", "beam", None),
        check_vma=False,
    )
```

```python
import functools

import jax
import jax.numpy as jnp
from jax import lax
from jax.experimental import pallas as pl
from jax.experimental.pallas import tpu as pltpu
from jax.sharding import PartitionSpec as P

TILE = 512
TAPS = 3
BLK = 16
RING = 4
QROWS = 32
EDGE = 8
ROWS = QROWS + EDGE
WIDTH = 2048
TILES = WIDTH // TILE
FULL = WIDTH + 2 * TILE
LANES = 512
SPANS = ((0, 16), (16, 32), (32, 40))
HBM = pl.BlockSpec(memory_space=pltpu.HBM)
VMEM = pl.BlockSpec(memory_space=pltpu.VMEM)
SMEM = pl.BlockSpec(memory_space=pltpu.SMEM)
IMAGE = pltpu.VMEM((2 * ROWS, WIDTH), jnp.float32)
PHASE_ROWS = ROWS + QROWS
PHASES = ((2, 2, PHASE_ROWS, TILE), (2, TILES, 2, PHASE_ROWS, 128))
MATRIX = pltpu.VMEM((TAPS * TILE, TILE), jnp.bfloat16)


def exchange(value, distance):
    count = lax.axis_size("grp")
    return lax.ppermute(value, "grp", [(i, i ^ distance) for i in range(count)])


def split(value):
    high = value.astype(jnp.bfloat16)
    low = (value - high.astype(jnp.float32)).astype(jnp.bfloat16)
    return high, low


def fetch(sems, pairs):
    copies = [pltpu.make_async_copy(a, b, sems.at[i]) for i, (a, b) in enumerate(pairs)]
    for copy in copies:
        copy.start()
    return copies


def range_products(high, low, t_high, t_low, full, count):
    rows = count * 2 * ROWS
    dot = functools.partial(jnp.dot, preferred_element_type=jnp.float32)
    full[:count, :, 5 * TILE :] = jnp.zeros((count, 2 * ROWS, TILE), jnp.float32)
    if count == 1:
        parts = [
            [part[0, :, m * TILE : (m + 1) * TILE] for m in range(TILES)] for part in (high, low)
        ]
        for t in range(TAPS):
            uses = [m for m in range(TILES) if m - t >= -1]
            n = len(uses) * rows
            a_high, a_low = ([part[m] for m in uses] for part in parts)
            at = slice(t * TILE, (t + 1) * TILE)
            both = dot(jnp.concatenate(a_high + a_low, 0), t_high[at, :])
            summed = both[:n] + both[n:] + dot(jnp.concatenate(a_high, 0), t_low[at, :])
            for i, m in enumerate(uses):
                to = slice((m - t + 1) * TILE, (m - t + 2) * TILE)
                value = summed[i * rows : (i + 1) * rows]
                full[0, :, to] = value if t == 0 or m == 0 else full[0, :, to] + value
        return
    for index in range(5):
        first = index - 1
        taps = [t for t in range(TAPS) if 0 <= first + t < TILES]
        k0, k1 = taps[0] * TILE, (taps[-1] + 1) * TILE
        a0, a1 = k0 + first * TILE, k1 + first * TILE
        a_high = high[:count, :, a0:a1].reshape(rows, a1 - a0)
        a_low = low[:count, :, a0:a1].reshape(rows, a1 - a0)
        summed = dot(a_high, t_high[k0:k1, :]) + (
            dot(a_high, t_low[k0:k1, :]) + dot(a_low, t_high[k0:k1, :])
        )
        full[:count, :, index * TILE : (index + 1) * TILE] = summed.reshape(count, 2 * ROWS, TILE)


def shifted(tiles):
    rows = tiles.shape[0]
    return [
        (tiles if k == 1 else pltpu.roll(tiles, (1 - k) % rows, 0))[8 : rows - 8] for k in range(4)
    ]


def unit(phases, e, row, count, lane):
    within, across = phases
    at = pl.ds(pl.multiple_of(lane % TILE, 128), LANES)
    n = lane // TILE
    c, s = (within[i, e, row : row + count, at] for i in range(2))
    cn, sn = (
        jnp.concatenate([across[i, n, e, row : row + count, :]] * (LANES // 128), 1)
        for i in range(2)
    )
    return c * cn - s * sn, s * cn + c * sn


def merge(section, block, lane, fulls, children, halves, offsets, w_ref, phases):
    r0, r1 = SPANS[block]
    out = [[None, None] for _ in halves]
    for full, e in zip(fulls, children):

        def rows_at(offset, row, count):
            start = pl.multiple_of(offset * TILE + lane, 128)
            return full[row : row + count, pl.ds(start, LANES)]

        parts = []
        for base in (0, ROWS):
            if block == 0:
                o = offsets[section, e, 0]
                tiles = [rows_at(o, base + 32, 8), rows_at(o, base, 24)]
            elif block == 1:
                tiles = [rows_at(offsets[section, e, 1], base + 8, 32)]
            else:
                after, before = offsets[section, e, 2], offsets[section, e, 3]
                row = lax.broadcasted_iota(jnp.int32, (EDGE, LANES), 0)
                middle = jnp.where(
                    row < 4, rows_at(after, base + 32, 8), rows_at(before, base + 32, 8)
                )
                tiles = [rows_at(after, base + 24, 8), middle, rows_at(before, base, 8)]
            parts.append(shifted(jnp.concatenate(tiles, 0) if len(tiles) > 1 else tiles[0]))
        cosine, sine = unit(phases, e, section * ROWS + r0, r1 - r0, lane)
        for i, h in enumerate(halves):
            w = [w_ref[section, h, e, k] for k in range(4)]
            real, imag = (
                (w[0] * part[0] + w[1] * part[1]) + (w[2] * part[2] + w[3] * part[3])
                for part in parts
            )
            new = (real * cosine - imag * sine, real * sine + imag * cosine)
            out[i] = [n if o is None else o + n for o, n in zip(out[i], new)]
    return out


def first_merges(fulls, children, halves, where, offsets, w_ref, phases, high, low):
    @pl.loop(0, WIDTH, step=LANES)
    def _(lane):
        at = pl.ds(pl.multiple_of(lane, 128), LANES)
        blocks = [
            merge(0, b, lane, fulls, children, halves, offsets, w_ref, phases)
            for b in range(3)
        ]
        row = lax.broadcasted_iota(jnp.int32, (EDGE, LANES), 0)
        keep = jnp.where(row < 4, where[3], where[2]) > 0
        for i in range(len(halves)):
            merged = jnp.concatenate(
                [
                    jnp.where(keep, blocks[b][i][comp], 0.0) if b == 2 else blocks[b][i][comp]
                    for comp in range(2)
                    for b in range(3)
                ],
                0,
            )
            high[i, :, at], low[i, :, at] = split(merged)


def second_merges(fulls, children, halves, offsets, w_ref, phases, outs):
    @pl.loop(0, WIDTH, step=LANES)
    def _(lane):
        at = pl.ds(pl.multiple_of(lane, 128), LANES)
        for b in range(2):
            r0, r1 = SPANS[b]
            merged = merge(1, b, lane, fulls, children, halves, offsets, w_ref, phases)
            for i in range(len(halves)):
                for comp in range(2):
                    outs[i][comp, r0:r1, at] = merged[i][comp]


def pack_kernel(
    rates_in, offs_in, where, image, q1, q3, tail, head, edges, rates, offs, sems
):
    copies = fetch(
        sems,
        [
            (image.at[:, 0:8], edges.at[0]), (image.at[:, 120:128], edges.at[1]),
            (rates_in.at[0], rates), (offs_in.at[0], offs),
        ]
        + [
            (image.at[:, pl.ds(pl.multiple_of((where[4] ^ d) * QROWS, QROWS), QROWS)], out)
            for d, out in ((1, q1), (3, q3))
        ],
    )
    lane = lax.broadcasted_iota(jnp.int32, (1, WIDTH), 1)

    def line(*values):
        out = jnp.zeros((1, WIDTH), jnp.float32)
        for i, value in enumerate(values):
            out = jnp.where(lane == i, value, out)
        return out

    for copy in copies[:4]:
        copy.wait()

    def offset(e, block):
        return offs[e, block].astype(jnp.float32)

    tail[0:2] = edges[1, 0, 6:8]
    tail[2:4] = edges[1, 1, 6:8]
    tail[4:5] = line(rates[0, 127], rates[1, 127], offset(0, 7), offset(1, 7))
    tail[5:8] = jnp.zeros((3, WIDTH), jnp.float32)
    head[0:4] = edges[0, 0, 0:4]
    head[4:8] = edges[0, 1, 0:4]
    head[8:9] = line(rates[0, 0], rates[0, 1], rates[1, 0], rates[1, 1], offset(0, 0), offset(1, 0))
    head[9:16] = jnp.zeros((7, WIDTH), jnp.float32)
    for copy in copies[4:]:
        copy.wait()


def rims_kernel(where, image, before, after, e0, p1, p3, stage, rows, sems):
    copies = []
    for d in range(RING):
        q = where[4] ^ d
        trail = pl.multiple_of(jnp.minimum(q * QROWS + QROWS, 120), 8)
        lead = pl.multiple_of(jnp.maximum(q * QROWS - 8, 0), 8)
        copies.append((image.at[:, pl.ds(trail, 8)], rows.at[d, 0]))
        copies.append((image.at[:, pl.ds(lead, 8)], rows.at[d, 1]))
    part = pl.ds(pl.multiple_of((where[4] ^ 2) * QROWS, QROWS), QROWS)
    copies = fetch(sems, copies + [(image.at[:, part], stage.at[:, :QROWS])])
    for copy in copies:
        copy.wait()
    for d, (out, r) in enumerate(((e0, 0), (p1, 0), (stage, QROWS), (p3, 0))):
        q = where[4] ^ d
        for comp in range(2):
            out[comp, r : r + 4] = jnp.where(
                q == 3, after[4 * comp : 4 * comp + 4], rows[d, 0, comp, 0:4]
            )
            out[comp, r + 4 : r + 6] = jnp.zeros((2, WIDTH), jnp.float32)
            out[comp, r + 6 : r + 8] = jnp.where(
                q == 0, before[2 * comp : 2 * comp + 2], rows[d, 1, comp, 6:8]
            )


def split_tiles(values, high, low):
    @pl.loop(0, TAPS * TILE, step=64)
    def _(row):
        at = pl.ds(pl.multiple_of(row, 64), 64)
        high[at], low[at] = split(values[at])


def fill(image, rim, high, low):
    rows = jnp.concatenate([image[...], rim[...]], 1)
    high[...], low[...] = split(rows.reshape(2 * ROWS, WIDTH))


def own_kernel(where, tiles, image, e0, full1_0, th, tl, main, high, low, t1, sems):
    part = pl.ds(pl.multiple_of(where[4] * QROWS, QROWS), QROWS)
    copies = fetch(sems, [(tiles.at[0], t1), (image.at[:, part], main)])
    copies[1].wait()
    fill(main, e0, high.at[0], low.at[0])
    copies[0].wait()
    split_tiles(t1, th, tl)
    range_products(high, low, th, tl, full1_0, 1)


def early_kernel(
    where, offsets, w_ref, full1_0, m1, e1, th1, tl1, tiles, within, across,
    full2, th2, tl2,
    high, low, full1, t2, sems,
):
    copies = fetch(sems, [(tiles.at[1], t2)])
    bit = where[0]
    fill(m1, e1, high.at[0], low.at[0])
    range_products(high, low, th1, tl1, full1, 1)
    first_merges(
        (full1_0.at[0], full1.at[0]), (bit, 1 - bit), (bit, 1 - bit),
        where, offsets, w_ref, (within, across), high, low,
    )
    copies[0].wait()
    split_tiles(t2, th2, tl2)
    range_products(high, low, th2, tl2, full2, 2)


def middle_kernel(
    where, offsets, w_ref, m2, m3, e3, full2, th1, tl1, th2, tl2, within, across,
    d2, full1, full2_2,
    high, low,
):
    phases = (within, across)
    bit, bit2 = where[0], where[1]
    high[0], low[0] = split(m2[...].reshape(2 * ROWS, WIDTH))
    fill(m3, e3, high.at[1], low.at[1])
    range_products(high, low, th1, tl1, full1, 2)
    first_merges(
        (full1.at[0], full1.at[1]), (bit, 1 - bit), (bit,),
        where, offsets, w_ref, phases, high, low,
    )
    range_products(high, low, th2, tl2, full2_2, 1)
    second_merges(
        (full2.at[0], full2_2.at[0]), (bit2, 1 - bit2), (1 - bit2,),
        offsets, w_ref, phases, (d2,),
    )


def late_kernel(
    where, offsets, w_ref, full1, full2, th2, tl2, within, across,
    d1, d3,
    high, low, full2_3,
):
    phases = (within, across)
    bit, bit2 = where[0], where[1]
    first_merges(
        (full1.at[0], full1.at[1]), (bit, 1 - bit), (1 - bit,),
        where, offsets, w_ref, phases, high, low,
    )
    range_products(high, low, th2, tl2, full2_3, 1)
    second_merges(
        (full2.at[1], full2_3.at[0]), (bit2, 1 - bit2), (bit2, 1 - bit2),
        offsets, w_ref, phases, (d1, d3),
    )


def rest_kernel(where, offsets, w_ref, full2, full2_2, within, across, result, d0, sems):
    bit2 = where[1]
    second_merges(
        (full2.at[0], full2_2.at[0]), (bit2, 1 - bit2), (bit2,),
        offsets, w_ref, (within, across), (d0,),
    )
    at = pl.ds(pl.multiple_of(where[4] * QROWS, QROWS), QROWS)
    for copy in fetch(sems, [(d0, result.at[:, at])]):
        copy.wait()


def place_kernel(distances, where, *refs):
    pieces, (out, stages, sems, out_sems) = refs[: len(distances)], refs[-4:]
    reads, writes = [], []
    for i, d in enumerate(distances):
        for n in range(2):
            at = pl.ds(pl.multiple_of((where[4] ^ d) * QROWS + 16 * n, 16), 16)
            half = stages.at[i, :, 16 * n : 16 * n + 16]
            reads.append((pieces[i].at[:, 16 * n : 16 * n + 16], half))
            writes.append((half, out.at[:, at]))
    reads = fetch(sems, reads)
    copies = []
    for i, pair in enumerate(writes):
        reads[i].wait()
        copies += fetch(out_sems.at[i : i + 1], [pair])
    for copy in copies:
        copy.wait()


def call(kernel, name, outs, in_specs, out_specs, scratch, flops, moved, aliases=None, vmem=8):
    return pl.pallas_call(
        kernel,
        out_shape=[jax.ShapeDtypeStruct(shape, kind) for shape, kind in outs],
        in_specs=in_specs,
        out_specs=out_specs,
        scratch_shapes=scratch,
        input_output_aliases=aliases or {},
        compiler_params=pltpu.CompilerParams(vmem_limit_bytes=vmem * 2**20),
        cost_estimate=pl.CostEstimate(flops=flops, bytes_accessed=moved, transcendentals=0),
        name=name,
    )


def halves_scratch(count):
    return [pltpu.VMEM((count, 2 * ROWS, WIDTH), jnp.bfloat16)] * 2


def full_scratch(count):
    return pltpu.VMEM((count, 2 * ROWS, FULL), jnp.float32)


def per_device(subimages, beam_weights, range_tiles, tile_offsets, phase_rates):
    f32, bf16 = jnp.float32, jnp.bfloat16
    dma = pltpu.SemaphoreType.DMA
    mine = lax.axis_index("grp") & 3
    beam = lax.axis_index("beam")
    beams = lax.axis_size("beam")
    image = subimages.reshape(2, RING * QROWS, WIDTH)
    first = jnp.logical_and(beam == 0, mine == 0)
    last = jnp.logical_and(beam == beams - 1, mine == 3)
    where = jnp.stack(
        [mine & 1, mine >> 1, 1 - first.astype(jnp.int32), 1 - last.astype(jnp.int32), mine]
    ).astype(jnp.int32)
    piece_shape = ((2, QROWS, WIDTH), f32)
    quarter_shape = ((2, ROWS, WIDTH), f32)
    q1, q3, tail, head = call(
        pack_kernel, "pack", [piece_shape, piece_shape, ((8, WIDTH), f32), ((16, WIDTH), f32)],
        [HBM] * 2 + [SMEM] + [HBM], [VMEM] * 4,
        [pltpu.VMEM((2, 2, 8, WIDTH), f32), pltpu.SMEM((2, 4 * QROWS), f32)]
        + [pltpu.SMEM((2, 8), jnp.int32), dma((6,))],
        10**6, 2**20, vmem=62,
    )(phase_rates, tile_offsets, where, image)
    m1 = exchange(q1, 1)
    m3 = exchange(q3, 3)
    before = lax.ppermute(tail, "beam", [(i, i + 1) for i in range(beams - 1)])
    after = lax.ppermute(head, "beam", [(i + 1, i) for i in range(beams - 1)])
    rim_shape = ((2, EDGE, WIDTH), f32)
    e0, p1, p3, q2 = call(
        rims_kernel, "rims", [rim_shape] * 3 + [quarter_shape],
        [SMEM, HBM, VMEM, VMEM], [VMEM] * 4,
        [pltpu.VMEM((RING, 2, 2, 8, WIDTH), f32), dma((9,))],
        10**6, 3 * 2**20,
    )(where, image, before, after)
    e1 = exchange(p1, 1)
    e3 = exchange(p3, 3)
    q2, m1, e0 = lax.optimization_barrier((q2, m1, e0))
    m2 = exchange(q2, 2)

    before_values, after_values = before[4, :4].reshape(2, 2), after[8, :6]
    line = jnp.concatenate([before_values[0][:, None], phase_rates[0], after_values[:4].reshape(2, 2)], 1)
    line = lax.dynamic_slice_in_dim(line, mine * QROWS, QROWS + 3, 1)
    rates_b = lax.dynamic_slice_in_dim(phase_rates[1], mine * QROWS, QROWS, 1)
    rates = jnp.concatenate([line[:, 1:], jnp.zeros((2, 5), f32), line[:, :1], rates_b], 1)
    offs = tile_offsets[0].astype(f32)
    line = jnp.concatenate([before_values[1][:, None], offs, after_values[4:][:, None]], 1)
    line = lax.dynamic_slice_in_dim(line, mine * 2, 4, 1).astype(jnp.int32)
    offs_a = jnp.stack([line[:, 1], line[:, 2], line[:, 3], line[:, 0]], 1)
    offs_b = jnp.pad(lax.dynamic_slice_in_dim(tile_offsets[1], mine * 2, 2, 1), ((0, 0), (0, 2)))
    offsets = jnp.clip(jnp.stack([offs_a, offs_b]), 0, 2)
    angles = rates[:, :, None] * (jnp.arange(TILE, dtype=f32) / TILE)
    within = jnp.stack([jnp.cos(angles), jnp.sin(angles)])
    angles = jnp.arange(TILES, dtype=f32)[:, None, None, None] * rates[:, :, None]
    angles = jnp.broadcast_to(angles, (TILES, 2, PHASE_ROWS, 128))
    across = jnp.stack([jnp.cos(angles), jnp.sin(angles)])

    scalars = (where, offsets, beam_weights)
    full_shape = (2 * ROWS, FULL)
    one, two = ((1, *full_shape), f32), ((2, *full_shape), f32)
    matrix_shape = ((TAPS * TILE, TILE), bf16)
    matrices = range_tiles.reshape(2, TAPS * TILE, TILE)
    matrix_f32 = pltpu.VMEM((TAPS * TILE, TILE), f32)
    full1_0, t1h, t1l = call(
        own_kernel, "own", [one, matrix_shape, matrix_shape], [SMEM] + [HBM] * 2 + [VMEM],
        [VMEM] * 3, [pltpu.VMEM(*piece_shape)] + halves_scratch(1) + [matrix_f32, dma((2,))],
        30 * 10**9, 8 * 2**20, vmem=16,
    )(where, matrices, image, e0)
    full2, t2h, t2l = call(
        early_kernel, "early", [two, matrix_shape, matrix_shape],
        [SMEM] * 3 + [VMEM] * 5 + [HBM] + [VMEM] * 2, [VMEM] * 3,
        halves_scratch(2) + [full_scratch(1), matrix_f32, dma((1,))],
        10**4, 10**4, vmem=28,
    )(*scalars, full1_0, m1, e1, t1h, t1l, matrices, within, across)
    d2, full1, full2_2 = call(
        middle_kernel, "middle", [piece_shape, two, one],
        [SMEM] * 3 + [VMEM] * 10, [VMEM] * 3, halves_scratch(2),
        9 * 10**9, 10 * 2**20, vmem=24,
    )(*scalars, m2, m3, e3, full2, t1h, t1l, t2h, t2l, within, across)
    r2 = exchange(d2, 2)
    d1, d3 = call(
        late_kernel, "late", [piece_shape] * 2, [SMEM] * 3 + [VMEM] * 6, [VMEM] * 2,
        halves_scratch(1) + [full_scratch(1)],
        7 * 10**9, 4 * 2**20, vmem=20,
    )(*scalars, full1, full2, t2h, t2l, within, across)
    r1 = exchange(d1, 1)
    r3 = exchange(d3, 3)
    (result,) = call(
        rest_kernel, "rest", [((2, RING * QROWS, WIDTH), f32)], [SMEM] * 3 + [VMEM] * 4, [HBM],
        [pltpu.VMEM(*piece_shape), dma((1,))],
        3 * 10**9, 3 * 2**20, vmem=12,
    )(*scalars, full2, full2_2, within, across)

    for distances, pieces, flops in (((2,), (r2,), 10**11), ((1, 3), (r1, r3), 10**5)):
        (result,) = call(
            functools.partial(place_kernel, distances), "place", [(result.shape, f32)],
            [SMEM] + [HBM] * (len(pieces) + 1), [HBM],
            [pltpu.VMEM((len(pieces), *piece_shape[0]), f32)] + [dma((2 * len(pieces),))] * 2,
            flops, 2**21, {1 + len(pieces): 0},
        )(where, *pieces, result)
    return result[:, None]


def solution(mesh):
    return jax.shard_map(
        per_device,
        mesh=mesh,
        in_specs=(
            P(None, "grp", "beam", None),
            P(),
            P(),
            P(None, None, "beam"),
            P(None, None, "beam"),
        ),
        out_specs=P(None, "grp", "beam", None),
        check_vma=False,
    )
```

```python
import functools

import jax
import jax.numpy as jnp
from jax import lax
from jax.experimental import pallas as pl
from jax.experimental.pallas import tpu as pltpu
from jax.sharding import PartitionSpec as P

TILE = 512
TAPS = 3
BLK = 16
RING = 4
QROWS = 32
EDGE = 8
ROWS = QROWS + EDGE
WIDTH = 2048
TILES = WIDTH // TILE
FULL = WIDTH + 2 * TILE
LANES = 512
SPANS = ((0, 16), (16, 32), (32, 40))
HBM = pl.BlockSpec(memory_space=pltpu.HBM)
VMEM = pl.BlockSpec(memory_space=pltpu.VMEM)
SMEM = pl.BlockSpec(memory_space=pltpu.SMEM)
IMAGE = pltpu.VMEM((2 * ROWS, WIDTH), jnp.float32)
PHASE_ROWS = ROWS + QROWS
PHASES = ((2, 2, PHASE_ROWS, TILE), (2, TILES, 2, PHASE_ROWS, 128))
MATRIX = pltpu.VMEM((TAPS * TILE, TILE), jnp.bfloat16)


def exchange(value, distance):
    count = lax.axis_size("grp")
    return lax.ppermute(value, "grp", [(i, i ^ distance) for i in range(count)])


def split(value):
    high = value.astype(jnp.bfloat16)
    low = (value - high.astype(jnp.float32)).astype(jnp.bfloat16)
    return high, low


def fetch(sems, pairs):
    copies = [pltpu.make_async_copy(a, b, sems.at[i]) for i, (a, b) in enumerate(pairs)]
    for copy in copies:
        copy.start()
    return copies


def range_products(high, low, t_high, t_low, full, count):
    rows = count * 2 * ROWS
    dot = functools.partial(jnp.dot, preferred_element_type=jnp.float32)
    full[:count, :, 5 * TILE :] = jnp.zeros((count, 2 * ROWS, TILE), jnp.float32)
    if count == 1:
        parts = [
            [part[0, :, m * TILE : (m + 1) * TILE] for m in range(TILES)] for part in (high, low)
        ]
        for t in range(TAPS):
            uses = [m for m in range(TILES) if m - t >= -1]
            n = len(uses) * rows
            a_high, a_low = ([part[m] for m in uses] for part in parts)
            at = slice(t * TILE, (t + 1) * TILE)
            both = dot(jnp.concatenate(a_high + a_low, 0), t_high[at, :])
            summed = both[:n] + both[n:] + dot(jnp.concatenate(a_high, 0), t_low[at, :])
            for i, m in enumerate(uses):
                to = slice((m - t + 1) * TILE, (m - t + 2) * TILE)
                value = summed[i * rows : (i + 1) * rows]
                full[0, :, to] = value if t == 0 or m == 0 else full[0, :, to] + value
        return
    for index in range(5):
        first = index - 1
        taps = [t for t in range(TAPS) if 0 <= first + t < TILES]
        k0, k1 = taps[0] * TILE, (taps[-1] + 1) * TILE
        a0, a1 = k0 + first * TILE, k1 + first * TILE
        a_high = high[:count, :, a0:a1].reshape(rows, a1 - a0)
        a_low = low[:count, :, a0:a1].reshape(rows, a1 - a0)
        summed = dot(a_high, t_high[k0:k1, :]) + (
            dot(a_high, t_low[k0:k1, :]) + dot(a_low, t_high[k0:k1, :])
        )
        full[:count, :, index * TILE : (index + 1) * TILE] = summed.reshape(count, 2 * ROWS, TILE)


def shifted(tiles):
    rows = tiles.shape[0]
    return [
        (tiles if k == 1 else pltpu.roll(tiles, (1 - k) % rows, 0))[8 : rows - 8] for k in range(4)
    ]


def unit(phases, e, row, count, lane):
    within, across = phases
    at = pl.ds(pl.multiple_of(lane % TILE, 128), LANES)
    n = lane // TILE
    c, s = (within[i, e, row : row + count, at] for i in range(2))
    cn, sn = (
        jnp.concatenate([across[i, n, e, row : row + count, :]] * (LANES // 128), 1)
        for i in range(2)
    )
    return c * cn - s * sn, s * cn + c * sn


def merge(section, block, lane, fulls, children, halves, offsets, w_ref, phases):
    r0, r1 = SPANS[block]
    out = [[None, None] for _ in halves]
    for full, e in zip(fulls, children):

        def rows_at(offset, row, count):
            start = pl.multiple_of(offset * TILE + lane, 128)
            return full[row : row + count, pl.ds(start, LANES)]

        parts = []
        for base in (0, ROWS):
            if block == 0:
                o = offsets[section, e, 0]
                tiles = [rows_at(o, base + 32, 8), rows_at(o, base, 24)]
            elif block == 1:
                tiles = [rows_at(offsets[section, e, 1], base + 8, 32)]
            else:
                after, before = offsets[section, e, 2], offsets[section, e, 3]
                row = lax.broadcasted_iota(jnp.int32, (EDGE, LANES), 0)
                middle = jnp.where(
                    row < 4, rows_at(after, base + 32, 8), rows_at(before, base + 32, 8)
                )
                tiles = [rows_at(after, base + 24, 8), middle, rows_at(before, base, 8)]
            parts.append(shifted(jnp.concatenate(tiles, 0) if len(tiles) > 1 else tiles[0]))
        cosine, sine = unit(phases, e, section * ROWS + r0, r1 - r0, lane)
        for i, h in enumerate(halves):
            w = [w_ref[section, h, e, k] for k in range(4)]
            real, imag = (
                (w[0] * part[0] + w[1] * part[1]) + (w[2] * part[2] + w[3] * part[3])
                for part in parts
            )
            new = (real * cosine - imag * sine, real * sine + imag * cosine)
            out[i] = [n if o is None else o + n for o, n in zip(out[i], new)]
    return out


def first_merges(fulls, children, halves, where, offsets, w_ref, phases, high, low):
    @pl.loop(0, WIDTH, step=LANES)
    def _(lane):
        at = pl.ds(pl.multiple_of(lane, 128), LANES)
        blocks = [
            merge(0, b, lane, fulls, children, halves, offsets, w_ref, phases)
            for b in range(3)
        ]
        row = lax.broadcasted_iota(jnp.int32, (EDGE, LANES), 0)
        keep = jnp.where(row < 4, where[3], where[2]) > 0
        for i in range(len(halves)):
            merged = jnp.concatenate(
                [
                    jnp.where(keep, blocks[b][i][comp], 0.0) if b == 2 else blocks[b][i][comp]
                    for comp in range(2)
                    for b in range(3)
                ],
                0,
            )
            high[i, :, at], low[i, :, at] = split(merged)


def second_merges(fulls, children, halves, offsets, w_ref, phases, outs):
    @pl.loop(0, WIDTH, step=LANES)
    def _(lane):
        at = pl.ds(pl.multiple_of(lane, 128), LANES)
        for b in range(2):
            r0, r1 = SPANS[b]
            merged = merge(1, b, lane, fulls, children, halves, offsets, w_ref, phases)
            for i in range(len(halves)):
                for comp in range(2):
                    outs[i][comp, r0:r1, at] = merged[i][comp]


def pack_kernel(
    rates_in, offs_in, where, image, q1, q3, tail, head, edges, rates, offs, sems
):
    copies = fetch(
        sems,
        [
            (image.at[:, 0:8], edges.at[0]), (image.at[:, 120:128], edges.at[1]),
            (rates_in.at[0], rates), (offs_in.at[0], offs),
        ]
        + [
            (image.at[:, pl.ds(pl.multiple_of((where[4] ^ d) * QROWS, QROWS), QROWS)], out)
            for d, out in ((1, q1), (3, q3))
        ],
    )
    for copy in copies[:4]:
        copy.wait()
    tail[0:2] = edges[1, 0, 6:8]
    tail[2:4] = edges[1, 1, 6:8]
    tail[4:8] = jnp.zeros((4, WIDTH), jnp.float32)
    head[0:4] = edges[0, 0, 0:4]
    head[4:8] = edges[0, 1, 0:4]
    head[8:16] = jnp.zeros((8, WIDTH), jnp.float32)
    for out, row in ((tail, 4), (head, 8)):
        for e in range(2):
            out[row + e : row + e + 1, 0:128] = rates[e : e + 1]
            out[row + e : row + e + 1, 128:136] = offs[e : e + 1].astype(jnp.float32)
    for copy in copies[4:]:
        copy.wait()


def rims_kernel(where, image, before, after, e0, p1, p3, stage, rows, sems):
    copies = []
    for d in range(RING):
        q = where[4] ^ d
        trail = pl.multiple_of(jnp.minimum(q * QROWS + QROWS, 120), 8)
        lead = pl.multiple_of(jnp.maximum(q * QROWS - 8, 0), 8)
        copies.append((image.at[:, pl.ds(trail, 8)], rows.at[d, 0]))
        copies.append((image.at[:, pl.ds(lead, 8)], rows.at[d, 1]))
    part = pl.ds(pl.multiple_of((where[4] ^ 2) * QROWS, QROWS), QROWS)
    copies = fetch(sems, copies + [(image.at[:, part], stage.at[:, :QROWS])])
    for copy in copies:
        copy.wait()
    for d, (out, r) in enumerate(((e0, 0), (p1, 0), (stage, QROWS), (p3, 0))):
        q = where[4] ^ d
        for comp in range(2):
            out[comp, r : r + 4] = jnp.where(
                q == 3, after[4 * comp : 4 * comp + 4], rows[d, 0, comp, 0:4]
            )
            out[comp, r + 4 : r + 6] = jnp.zeros((2, WIDTH), jnp.float32)
            out[comp, r + 6 : r + 8] = jnp.where(
                q == 0, before[2 * comp : 2 * comp + 2], rows[d, 1, comp, 6:8]
            )


def split_tiles(values, high, low):
    @pl.loop(0, TAPS * TILE, step=64)
    def _(row):
        at = pl.ds(pl.multiple_of(row, 64), 64)
        high[at], low[at] = split(values[at])


def fill(image, rim, high, low):
    rows = jnp.concatenate([image[...], rim[...]], 1)
    high[...], low[...] = split(rows.reshape(2 * ROWS, WIDTH))


def own_kernel(where, tiles, image, e0, full1_0, th, tl, main, high, low, t1, sems):
    part = pl.ds(pl.multiple_of(where[4] * QROWS, QROWS), QROWS)
    copies = fetch(sems, [(tiles.at[0], t1), (image.at[:, part], main)])
    copies[1].wait()
    fill(main, e0, high.at[0], low.at[0])
    copies[0].wait()
    split_tiles(t1, th, tl)
    range_products(high, low, th, tl, full1_0, 1)


def early_kernel(
    where, offsets, w_ref, full1_0, m1, e1, th1, tl1, tiles, within, across,
    full2, th2, tl2,
    high, low, full1, t2, sems,
):
    copies = fetch(sems, [(tiles.at[1], t2)])
    bit = where[0]
    fill(m1, e1, high.at[0], low.at[0])
    range_products(high, low, th1, tl1, full1, 1)
    first_merges(
        (full1_0.at[0], full1.at[0]), (bit, 1 - bit), (bit, 1 - bit),
        where, offsets, w_ref, (within, across), high, low,
    )
    copies[0].wait()
    split_tiles(t2, th2, tl2)
    range_products(high, low, th2, tl2, full2, 2)


def middle_kernel(
    where, offsets, w_ref, m2, m3, e3, full2, th1, tl1, th2, tl2, within, across,
    d2, full1, full2_2,
    high, low,
):
    phases = (within, across)
    bit, bit2 = where[0], where[1]
    high[0], low[0] = split(m2[...].reshape(2 * ROWS, WIDTH))
    fill(m3, e3, high.at[1], low.at[1])
    range_products(high, low, th1, tl1, full1, 2)
    first_merges(
        (full1.at[0], full1.at[1]), (bit, 1 - bit), (bit,),
        where, offsets, w_ref, phases, high, low,
    )
    range_products(high, low, th2, tl2, full2_2, 1)
    second_merges(
        (full2.at[0], full2_2.at[0]), (bit2, 1 - bit2), (1 - bit2,),
        offsets, w_ref, phases, (d2,),
    )


def late_kernel(
    where, offsets, w_ref, full1, full2, th2, tl2, within, across,
    d1, d3,
    high, low, full2_3,
):
    phases = (within, across)
    bit, bit2 = where[0], where[1]
    first_merges(
        (full1.at[0], full1.at[1]), (bit, 1 - bit), (1 - bit,),
        where, offsets, w_ref, phases, high, low,
    )
    range_products(high, low, th2, tl2, full2_3, 1)
    second_merges(
        (full2.at[1], full2_3.at[0]), (bit2, 1 - bit2), (bit2, 1 - bit2),
        offsets, w_ref, phases, (d1, d3),
    )


def rest_kernel(where, offsets, w_ref, full2, full2_2, within, across, result, d0, sems):
    bit2 = where[1]
    second_merges(
        (full2.at[0], full2_2.at[0]), (bit2, 1 - bit2), (bit2,),
        offsets, w_ref, (within, across), (d0,),
    )
    at = pl.ds(pl.multiple_of(where[4] * QROWS, QROWS), QROWS)
    for copy in fetch(sems, [(d0, result.at[:, at])]):
        copy.wait()


def place_kernel(distances, where, *refs):
    pieces, (out, sems) = refs[: len(distances)], refs[-2:]
    copies = []
    for piece, d in zip(pieces, distances):
        for n in (0, 16):
            at = pl.ds(pl.multiple_of((where[4] ^ d) * QROWS + n, 16), 16)
            copies += [(piece.at[c, n : n + 16], out.at[c, at]) for c in range(2)]
    for copy in fetch(sems, copies):
        copy.wait()


def call(kernel, name, outs, in_specs, out_specs, scratch, flops, moved, aliases=None, vmem=8):
    return pl.pallas_call(
        kernel,
        out_shape=[jax.ShapeDtypeStruct(shape, kind) for shape, kind in outs],
        in_specs=in_specs,
        out_specs=out_specs,
        scratch_shapes=scratch,
        input_output_aliases=aliases or {},
        compiler_params=pltpu.CompilerParams(vmem_limit_bytes=vmem * 2**20),
        cost_estimate=pl.CostEstimate(flops=flops, bytes_accessed=moved, transcendentals=0),
        name=name,
    )


def halves_scratch(count):
    return [pltpu.VMEM((count, 2 * ROWS, WIDTH), jnp.bfloat16)] * 2


def full_scratch(count):
    return pltpu.VMEM((count, 2 * ROWS, FULL), jnp.float32)


def per_device(subimages, beam_weights, range_tiles, tile_offsets, phase_rates):
    f32, bf16 = jnp.float32, jnp.bfloat16
    dma = pltpu.SemaphoreType.DMA
    mine = lax.axis_index("grp") & 3
    beam = lax.axis_index("beam")
    beams = lax.axis_size("beam")
    image = subimages.reshape(2, RING * QROWS, WIDTH)
    first = jnp.logical_and(beam == 0, mine == 0)
    last = jnp.logical_and(beam == beams - 1, mine == 3)
    where = jnp.stack(
        [mine & 1, mine >> 1, 1 - first.astype(jnp.int32), 1 - last.astype(jnp.int32), mine]
    ).astype(jnp.int32)
    piece_shape = ((2, QROWS, WIDTH), f32)
    quarter_shape = ((2, ROWS, WIDTH), f32)
    q1, q3, tail, head = call(
        pack_kernel, "pack", [piece_shape, piece_shape, ((8, WIDTH), f32), ((16, WIDTH), f32)],
        [HBM] * 2 + [SMEM] + [HBM], [VMEM] * 4,
        [pltpu.VMEM((2, 2, 8, WIDTH), f32), pltpu.VMEM((2, 4 * QROWS), f32)]
        + [pltpu.VMEM((2, 8), jnp.int32), dma((6,))],
        10**6, 2**20, vmem=60,
    )(phase_rates, tile_offsets, where, image)
    m1 = exchange(q1, 1)
    m3 = exchange(q3, 3)
    before = lax.ppermute(tail, "beam", [(i, i + 1) for i in range(beams - 1)])
    after = lax.ppermute(head, "beam", [(i + 1, i) for i in range(beams - 1)])
    rim_shape = ((2, EDGE, WIDTH), f32)
    e0, p1, p3, q2 = call(
        rims_kernel, "rims", [rim_shape] * 3 + [quarter_shape],
        [SMEM, HBM, VMEM, VMEM], [VMEM] * 4,
        [pltpu.VMEM((RING, 2, 2, 8, WIDTH), f32), dma((9,))],
        10**6, 3 * 2**20,
    )(where, image, before, after)
    e1 = exchange(p1, 1)
    e3 = exchange(p3, 3)
    q2, e0 = lax.optimization_barrier((q2, e0))
    m2 = exchange(q2, 2)

    line = jnp.concatenate([before[4:6, 127:128], phase_rates[0], after[8:10, :2]], 1)
    line = lax.dynamic_slice_in_dim(line, mine * QROWS, QROWS + 3, 1)
    rates_b = lax.dynamic_slice_in_dim(phase_rates[1], mine * QROWS, QROWS, 1)
    rates = jnp.concatenate([line[:, 1:], jnp.zeros((2, 5), f32), line[:, :1], rates_b], 1)
    offs = tile_offsets[0].astype(f32)
    line = jnp.concatenate([before[4:6, 135:136], offs, after[8:10, 128:129]], 1)
    line = lax.dynamic_slice_in_dim(line, mine * 2, 4, 1).astype(jnp.int32)
    offs_a = jnp.stack([line[:, 1], line[:, 2], line[:, 3], line[:, 0]], 1)
    offs_b = jnp.pad(lax.dynamic_slice_in_dim(tile_offsets[1], mine * 2, 2, 1), ((0, 0), (0, 2)))
    offsets = jnp.clip(jnp.stack([offs_a, offs_b]), 0, 2)
    angles = rates[:, :, None] * (jnp.arange(TILE, dtype=f32) / TILE)
    within = jnp.stack([jnp.cos(angles), jnp.sin(angles)])
    angles = jnp.arange(TILES, dtype=f32)[:, None, None, None] * rates[:, :, None]
    angles = jnp.broadcast_to(angles, (TILES, 2, PHASE_ROWS, 128))
    across = jnp.stack([jnp.cos(angles), jnp.sin(angles)])

    scalars = (where, offsets, beam_weights)
    full_shape = (2 * ROWS, FULL)
    one, two = ((1, *full_shape), f32), ((2, *full_shape), f32)
    matrix_shape = ((TAPS * TILE, TILE), bf16)
    matrices = range_tiles.reshape(2, TAPS * TILE, TILE)
    matrix_f32 = pltpu.VMEM((TAPS * TILE, TILE), f32)
    full1_0, t1h, t1l = call(
        own_kernel, "own", [one, matrix_shape, matrix_shape], [SMEM] + [HBM] * 2 + [VMEM],
        [VMEM] * 3, [pltpu.VMEM(*piece_shape)] + halves_scratch(1) + [matrix_f32, dma((2,))],
        30 * 10**9, 8 * 2**20, vmem=16,
    )(where, matrices, image, e0)
    full2, t2h, t2l = call(
        early_kernel, "early", [two, matrix_shape, matrix_shape],
        [SMEM] * 3 + [VMEM] * 5 + [HBM] + [VMEM] * 2, [VMEM] * 3,
        halves_scratch(2) + [full_scratch(1), matrix_f32, dma((1,))],
        10**4, 10**4, vmem=28,
    )(*scalars, full1_0, m1, e1, t1h, t1l, matrices, within, across)
    d2, full1, full2_2 = call(
        middle_kernel, "middle", [piece_shape, two, one],
        [SMEM] * 3 + [VMEM] * 10, [VMEM] * 3, halves_scratch(2),
        9 * 10**9, 10 * 2**20, vmem=24,
    )(*scalars, m2, m3, e3, full2, t1h, t1l, t2h, t2l, within, across)
    r2 = exchange(d2, 2)
    d1, d3 = call(
        late_kernel, "late", [piece_shape] * 2, [SMEM] * 3 + [VMEM] * 6, [VMEM] * 2,
        halves_scratch(1) + [full_scratch(1)],
        7 * 10**9, 4 * 2**20, vmem=20,
    )(*scalars, full1, full2, t2h, t2l, within, across)
    r1 = exchange(d1, 1)
    r3 = exchange(d3, 3)
    (result,) = call(
        rest_kernel, "rest", [((2, RING * QROWS, WIDTH), f32)], [SMEM] * 3 + [VMEM] * 4, [HBM],
        [pltpu.VMEM(*piece_shape), dma((1,))],
        3 * 10**9, 3 * 2**20, vmem=12,
    )(*scalars, full2, full2_2, within, across)

    for distances, pieces, flops in (((2,), (r2,), 10**11), ((1, 3), (r1, r3), 10**5)):
        (result,) = call(
            functools.partial(place_kernel, distances), "place", [(result.shape, f32)],
            [SMEM] + [VMEM] * len(pieces) + [HBM], [HBM], [dma((4 * len(pieces),))],
            flops, 2**21, {1 + len(pieces): 0},
        )(where, *pieces, result)
    return result[:, None]


def solution(mesh):
    return jax.shard_map(
        per_device,
        mesh=mesh,
        in_specs=(
            P(None, "grp", "beam", None),
            P(),
            P(),
            P(None, None, "beam"),
            P(None, None, "beam"),
        ),
        out_specs=P(None, "grp", "beam", None),
        check_vma=False,
    )
```

```python
import functools

import jax
import jax.numpy as jnp
from jax import lax
from jax.experimental import pallas as pl
from jax.experimental.pallas import tpu as pltpu
from jax.sharding import PartitionSpec as P

TILE = 512
TAPS = 3
BLK = 16
RING = 4
QROWS = 32
EDGE = 8
ROWS = QROWS + EDGE
WIDTH = 2048
TILES = WIDTH // TILE
FULL = WIDTH + 2 * TILE
LANES = 512
SPANS = ((0, 16), (16, 32), (32, 40))
HBM = pl.BlockSpec(memory_space=pltpu.HBM)
VMEM = pl.BlockSpec(memory_space=pltpu.VMEM)
SMEM = pl.BlockSpec(memory_space=pltpu.SMEM)
IMAGE = pltpu.VMEM((2 * ROWS, WIDTH), jnp.float32)
PHASE_ROWS = ROWS + QROWS
PHASES = ((2, 2, PHASE_ROWS, TILE), (2, TILES, 2, PHASE_ROWS, 128))
MATRIX = pltpu.VMEM((TAPS * TILE, TILE), jnp.bfloat16)


def exchange(value, distance):
    count = lax.axis_size("grp")
    return lax.ppermute(value, "grp", [(i, i ^ distance) for i in range(count)])


def split(value):
    high = value.astype(jnp.bfloat16)
    low = (value - high.astype(jnp.float32)).astype(jnp.bfloat16)
    return high, low


def fetch(sems, pairs):
    copies = [pltpu.make_async_copy(a, b, sems.at[i]) for i, (a, b) in enumerate(pairs)]
    for copy in copies:
        copy.start()
    return copies


def range_products(high, low, t_high, t_low, full, count):
    rows = count * 2 * ROWS
    dot = functools.partial(jnp.dot, preferred_element_type=jnp.float32)
    full[:count, :, 5 * TILE :] = jnp.zeros((count, 2 * ROWS, TILE), jnp.float32)
    if count == 1:
        parts = [
            [part[0, :, m * TILE : (m + 1) * TILE] for m in range(TILES)] for part in (high, low)
        ]
        for t in range(TAPS):
            uses = [m for m in range(TILES) if m - t >= -1]
            n = len(uses) * rows
            a_high, a_low = ([part[m] for m in uses] for part in parts)
            at = slice(t * TILE, (t + 1) * TILE)
            both = dot(jnp.concatenate(a_high + a_low, 0), t_high[at, :])
            summed = both[:n] + both[n:] + dot(jnp.concatenate(a_high, 0), t_low[at, :])
            for i, m in enumerate(uses):
                to = slice((m - t + 1) * TILE, (m - t + 2) * TILE)
                value = summed[i * rows : (i + 1) * rows]
                full[0, :, to] = value if t == 0 or m == 0 else full[0, :, to] + value
        return
    for index in range(5):
        first = index - 1
        taps = [t for t in range(TAPS) if 0 <= first + t < TILES]
        k0, k1 = taps[0] * TILE, (taps[-1] + 1) * TILE
        a0, a1 = k0 + first * TILE, k1 + first * TILE
        a_high = high[:count, :, a0:a1].reshape(rows, a1 - a0)
        a_low = low[:count, :, a0:a1].reshape(rows, a1 - a0)
        summed = dot(a_high, t_high[k0:k1, :]) + (
            dot(a_high, t_low[k0:k1, :]) + dot(a_low, t_high[k0:k1, :])
        )
        full[:count, :, index * TILE : (index + 1) * TILE] = summed.reshape(count, 2 * ROWS, TILE)


def shifted(tiles):
    rows = tiles.shape[0]
    return [
        (tiles if k == 1 else pltpu.roll(tiles, (1 - k) % rows, 0))[8 : rows - 8] for k in range(4)
    ]


def unit(phases, e, row, count, lane):
    within, across = phases
    at = pl.ds(pl.multiple_of(lane % TILE, 128), LANES)
    n = lane // TILE
    c, s = (within[i, e, row : row + count, at] for i in range(2))
    cn, sn = (
        jnp.concatenate([across[i, n, e, row : row + count, :]] * (LANES // 128), 1)
        for i in range(2)
    )
    return c * cn - s * sn, s * cn + c * sn


def merge(section, block, lane, fulls, children, halves, offsets, w_ref, phases):
    r0, r1 = SPANS[block]
    out = [[None, None] for _ in halves]
    for full, e in zip(fulls, children):

        def rows_at(offset, row, count):
            start = pl.multiple_of(offset * TILE + lane, 128)
            return full[row : row + count, pl.ds(start, LANES)]

        parts = []
        for base in (0, ROWS):
            if block == 0:
                o = offsets[section, e, 0]
                tiles = [rows_at(o, base + 32, 8), rows_at(o, base, 24)]
            elif block == 1:
                tiles = [rows_at(offsets[section, e, 1], base + 8, 32)]
            else:
                after, before = offsets[section, e, 2], offsets[section, e, 3]
                row = lax.broadcasted_iota(jnp.int32, (EDGE, LANES), 0)
                middle = jnp.where(
                    row < 4, rows_at(after, base + 32, 8), rows_at(before, base + 32, 8)
                )
                tiles = [rows_at(after, base + 24, 8), middle, rows_at(before, base, 8)]
            parts.append(shifted(jnp.concatenate(tiles, 0) if len(tiles) > 1 else tiles[0]))
        cosine, sine = unit(phases, e, section * ROWS + r0, r1 - r0, lane)
        for i, h in enumerate(halves):
            w = [w_ref[section, h, e, k] for k in range(4)]
            real, imag = (
                (w[0] * part[0] + w[1] * part[1]) + (w[2] * part[2] + w[3] * part[3])
                for part in parts
            )
            new = (real * cosine - imag * sine, real * sine + imag * cosine)
            out[i] = [n if o is None else o + n for o, n in zip(out[i], new)]
    return out


def first_merges(fulls, children, halves, where, offsets, w_ref, phases, high, low):
    @pl.loop(0, WIDTH, step=LANES)
    def _(lane):
        at = pl.ds(pl.multiple_of(lane, 128), LANES)
        blocks = [
            merge(0, b, lane, fulls, children, halves, offsets, w_ref, phases)
            for b in range(3)
        ]
        row = lax.broadcasted_iota(jnp.int32, (EDGE, LANES), 0)
        keep = jnp.where(row < 4, where[3], where[2]) > 0
        for i in range(len(halves)):
            merged = jnp.concatenate(
                [
                    jnp.where(keep, blocks[b][i][comp], 0.0) if b == 2 else blocks[b][i][comp]
                    for comp in range(2)
                    for b in range(3)
                ],
                0,
            )
            high[i, :, at], low[i, :, at] = split(merged)


def second_merges(fulls, children, halves, offsets, w_ref, phases, outs):
    @pl.loop(0, WIDTH, step=LANES)
    def _(lane):
        at = pl.ds(pl.multiple_of(lane, 128), LANES)
        for b in range(2):
            r0, r1 = SPANS[b]
            merged = merge(1, b, lane, fulls, children, halves, offsets, w_ref, phases)
            for i in range(len(halves)):
                for comp in range(2):
                    outs[i][comp, r0:r1, at] = merged[i][comp]


def pack_kernel(
    rates_in, offs_in, where, image, q1, q3, tail, head, edges, rates, offs, sems
):
    copies = fetch(
        sems,
        [
            (image.at[:, 0:8], edges.at[0]), (image.at[:, 120:128], edges.at[1]),
            (rates_in.at[0], rates), (offs_in.at[0], offs),
        ]
        + [
            (image.at[:, pl.ds(pl.multiple_of((where[4] ^ d) * QROWS, QROWS), QROWS)], out)
            for d, out in ((1, q1), (3, q3))
        ],
    )
    for copy in copies[:4]:
        copy.wait()
    tail[0:2] = edges[1, 0, 6:8]
    tail[2:4] = edges[1, 1, 6:8]
    tail[4:8] = jnp.zeros((4, WIDTH), jnp.float32)
    head[0:4] = edges[0, 0, 0:4]
    head[4:8] = edges[0, 1, 0:4]
    head[8:16] = jnp.zeros((8, WIDTH), jnp.float32)
    for out, row in ((tail, 4), (head, 8)):
        for e in range(2):
            out[row + e : row + e + 1, 0:128] = rates[e : e + 1]
            out[row + e : row + e + 1, 128:136] = offs[e : e + 1].astype(jnp.float32)
    for copy in copies[4:]:
        copy.wait()


def rims_kernel(where, image, before, after, e0, p1, p3, stage, rows, sems):
    copies = []
    for d in range(RING):
        q = where[4] ^ d
        trail = pl.multiple_of(jnp.minimum(q * QROWS + QROWS, 120), 8)
        lead = pl.multiple_of(jnp.maximum(q * QROWS - 8, 0), 8)
        copies.append((image.at[:, pl.ds(trail, 8)], rows.at[d, 0]))
        copies.append((image.at[:, pl.ds(lead, 8)], rows.at[d, 1]))
    part = pl.ds(pl.multiple_of((where[4] ^ 2) * QROWS, QROWS), QROWS)
    copies = fetch(sems, copies + [(image.at[:, part], stage.at[:, :QROWS])])
    for copy in copies:
        copy.wait()
    for d, (out, r) in enumerate(((e0, 0), (p1, 0), (stage, QROWS), (p3, 0))):
        q = where[4] ^ d
        for comp in range(2):
            out[comp, r : r + 4] = jnp.where(
                q == 3, after[4 * comp : 4 * comp + 4], rows[d, 0, comp, 0:4]
            )
            out[comp, r + 4 : r + 6] = jnp.zeros((2, WIDTH), jnp.float32)
            out[comp, r + 6 : r + 8] = jnp.where(
                q == 0, before[2 * comp : 2 * comp + 2], rows[d, 1, comp, 6:8]
            )


def split_tiles(values, high, low):
    @pl.loop(0, TAPS * TILE, step=64)
    def _(row):
        at = pl.ds(pl.multiple_of(row, 64), 64)
        high[at], low[at] = split(values[at])


def fill(image, rim, high, low):
    rows = jnp.concatenate([image[...], rim[...]], 1)
    high[...], low[...] = split(rows.reshape(2 * ROWS, WIDTH))


def own_kernel(where, tiles, image, e0, full1_0, th, tl, main, high, low, t1, sems):
    part = pl.ds(pl.multiple_of(where[4] * QROWS, QROWS), QROWS)
    copies = fetch(sems, [(tiles.at[0], t1), (image.at[:, part], main)])
    copies[1].wait()
    fill(main, e0, high.at[0], low.at[0])
    copies[0].wait()
    split_tiles(t1, th, tl)
    range_products(high, low, th, tl, full1_0, 1)


def early_kernel(
    where, offsets, w_ref, full1_0, m1, e1, th1, tl1, tiles, within, across,
    full2, th2, tl2,
    high, low, full1, t2, sems,
):
    copies = fetch(sems, [(tiles.at[1], t2)])
    bit = where[0]
    fill(m1, e1, high.at[0], low.at[0])
    range_products(high, low, th1, tl1, full1, 1)
    first_merges(
        (full1_0.at[0], full1.at[0]), (bit, 1 - bit), (bit, 1 - bit),
        where, offsets, w_ref, (within, across), high, low,
    )
    copies[0].wait()
    split_tiles(t2, th2, tl2)
    range_products(high, low, th2, tl2, full2, 2)


def third_kernel(m3, e3, th1, tl1, full1_3, high, low):
    fill(m3, e3, high.at[0], low.at[0])
    range_products(high, low, th1, tl1, full1_3, 1)


def middle_kernel(
    where, offsets, w_ref, m2, full1_3, full2, th1, tl1, th2, tl2, within, across,
    d2, full1_2, full2_2,
    high, low,
):
    phases = (within, across)
    bit, bit2 = where[0], where[1]
    high[0], low[0] = split(m2[...].reshape(2 * ROWS, WIDTH))
    range_products(high, low, th1, tl1, full1_2, 1)
    first_merges(
        (full1_2.at[0], full1_3.at[0]), (bit, 1 - bit), (bit,),
        where, offsets, w_ref, phases, high, low,
    )
    range_products(high, low, th2, tl2, full2_2, 1)
    second_merges(
        (full2.at[0], full2_2.at[0]), (bit2, 1 - bit2), (1 - bit2,),
        offsets, w_ref, phases, (d2,),
    )


def late_kernel(
    where, offsets, w_ref, full1_2, full1_3, full2, th2, tl2, within, across,
    d1, d3,
    high, low, full2_3,
):
    phases = (within, across)
    bit, bit2 = where[0], where[1]
    first_merges(
        (full1_2.at[0], full1_3.at[0]), (bit, 1 - bit), (1 - bit,),
        where, offsets, w_ref, phases, high, low,
    )
    range_products(high, low, th2, tl2, full2_3, 1)
    second_merges(
        (full2.at[1], full2_3.at[0]), (bit2, 1 - bit2), (bit2, 1 - bit2),
        offsets, w_ref, phases, (d1, d3),
    )


def rest_kernel(where, offsets, w_ref, full2, full2_2, within, across, result, d0, sems):
    bit2 = where[1]
    second_merges(
        (full2.at[0], full2_2.at[0]), (bit2, 1 - bit2), (bit2,),
        offsets, w_ref, (within, across), (d0,),
    )
    at = pl.ds(pl.multiple_of(where[4] * QROWS, QROWS), QROWS)
    for copy in fetch(sems, [(d0, result.at[:, at])]):
        copy.wait()


def place_kernel(distances, where, *refs):
    pieces, (out, sems) = refs[: len(distances)], refs[-2:]
    copies = []
    for piece, d in zip(pieces, distances):
        for n in (0, 16):
            at = pl.ds(pl.multiple_of((where[4] ^ d) * QROWS + n, 16), 16)
            copies += [(piece.at[c, n : n + 16], out.at[c, at]) for c in range(2)]
    for copy in fetch(sems, copies):
        copy.wait()


def call(kernel, name, outs, in_specs, out_specs, scratch, flops, moved, aliases=None, vmem=8):
    return pl.pallas_call(
        kernel,
        out_shape=[jax.ShapeDtypeStruct(shape, kind) for shape, kind in outs],
        in_specs=in_specs,
        out_specs=out_specs,
        scratch_shapes=scratch,
        input_output_aliases=aliases or {},
        compiler_params=pltpu.CompilerParams(vmem_limit_bytes=vmem * 2**20),
        cost_estimate=pl.CostEstimate(flops=flops, bytes_accessed=moved, transcendentals=0),
        name=name,
    )


def halves_scratch(count):
    return [pltpu.VMEM((count, 2 * ROWS, WIDTH), jnp.bfloat16)] * 2


def full_scratch(count):
    return pltpu.VMEM((count, 2 * ROWS, FULL), jnp.float32)


def per_device(subimages, beam_weights, range_tiles, tile_offsets, phase_rates):
    f32, bf16 = jnp.float32, jnp.bfloat16
    dma = pltpu.SemaphoreType.DMA
    mine = lax.axis_index("grp") & 3
    beam = lax.axis_index("beam")
    beams = lax.axis_size("beam")
    image = subimages.reshape(2, RING * QROWS, WIDTH)
    first = jnp.logical_and(beam == 0, mine == 0)
    last = jnp.logical_and(beam == beams - 1, mine == 3)
    where = jnp.stack(
        [mine & 1, mine >> 1, 1 - first.astype(jnp.int32), 1 - last.astype(jnp.int32), mine]
    ).astype(jnp.int32)
    piece_shape = ((2, QROWS, WIDTH), f32)
    quarter_shape = ((2, ROWS, WIDTH), f32)
    q1, q3, tail, head = call(
        pack_kernel, "pack", [piece_shape, piece_shape, ((8, WIDTH), f32), ((16, WIDTH), f32)],
        [HBM] * 2 + [SMEM] + [HBM], [VMEM] * 4,
        [pltpu.VMEM((2, 2, 8, WIDTH), f32), pltpu.VMEM((2, 4 * QROWS), f32)]
        + [pltpu.VMEM((2, 8), jnp.int32), dma((6,))],
        10**6, 2**20, vmem=60,
    )(phase_rates, tile_offsets, where, image)
    m1 = exchange(q1, 1)
    m3 = exchange(q3, 3)
    before = lax.ppermute(tail, "beam", [(i, i + 1) for i in range(beams - 1)])
    after = lax.ppermute(head, "beam", [(i + 1, i) for i in range(beams - 1)])
    rim_shape = ((2, EDGE, WIDTH), f32)
    e0, p1, p3, q2 = call(
        rims_kernel, "rims", [rim_shape] * 3 + [quarter_shape],
        [SMEM, HBM, VMEM, VMEM], [VMEM] * 4,
        [pltpu.VMEM((RING, 2, 2, 8, WIDTH), f32), dma((9,))],
        10**6, 3 * 2**20,
    )(where, image, before, after)
    e1 = exchange(p1, 1)
    e3 = exchange(p3, 3)
    q2, e0 = lax.optimization_barrier((q2, e0))
    m2 = exchange(q2, 2)

    line = jnp.concatenate([before[4:6, 127:128], phase_rates[0], after[8:10, :2]], 1)
    line = lax.dynamic_slice_in_dim(line, mine * QROWS, QROWS + 3, 1)
    rates_b = lax.dynamic_slice_in_dim(phase_rates[1], mine * QROWS, QROWS, 1)
    rates = jnp.concatenate([line[:, 1:], jnp.zeros((2, 5), f32), line[:, :1], rates_b], 1)
    offs = tile_offsets[0].astype(f32)
    line = jnp.concatenate([before[4:6, 135:136], offs, after[8:10, 128:129]], 1)
    line = lax.dynamic_slice_in_dim(line, mine * 2, 4, 1).astype(jnp.int32)
    offs_a = jnp.stack([line[:, 1], line[:, 2], line[:, 3], line[:, 0]], 1)
    offs_b = jnp.pad(lax.dynamic_slice_in_dim(tile_offsets[1], mine * 2, 2, 1), ((0, 0), (0, 2)))
    offsets = jnp.clip(jnp.stack([offs_a, offs_b]), 0, 2)
    angles = rates[:, :, None] * (jnp.arange(TILE, dtype=f32) / TILE)
    within = jnp.stack([jnp.cos(angles), jnp.sin(angles)])
    angles = jnp.arange(TILES, dtype=f32)[:, None, None, None] * rates[:, :, None]
    angles = jnp.broadcast_to(angles, (TILES, 2, PHASE_ROWS, 128))
    across = jnp.stack([jnp.cos(angles), jnp.sin(angles)])

    scalars = (where, offsets, beam_weights)
    full_shape = (2 * ROWS, FULL)
    one, two = ((1, *full_shape), f32), ((2, *full_shape), f32)
    matrix_shape = ((TAPS * TILE, TILE), bf16)
    matrices = range_tiles.reshape(2, TAPS * TILE, TILE)
    matrix_f32 = pltpu.VMEM((TAPS * TILE, TILE), f32)
    full1_0, t1h, t1l = call(
        own_kernel, "own", [one, matrix_shape, matrix_shape], [SMEM] + [HBM] * 2 + [VMEM],
        [VMEM] * 3, [pltpu.VMEM(*piece_shape)] + halves_scratch(1) + [matrix_f32, dma((2,))],
        30 * 10**9, 8 * 2**20, vmem=16,
    )(where, matrices, image, e0)
    full2, t2h, t2l = call(
        early_kernel, "early", [two, matrix_shape, matrix_shape],
        [SMEM] * 3 + [VMEM] * 5 + [HBM] + [VMEM] * 2, [VMEM] * 3,
        halves_scratch(2) + [full_scratch(1), matrix_f32, dma((1,))],
        10**4, 10**4, vmem=28,
    )(*scalars, full1_0, m1, e1, t1h, t1l, matrices, within, across)
    (full1_3,) = call(
        third_kernel, "third", [one], [VMEM] * 4, [VMEM], halves_scratch(1), 10**4, 10**4, vmem=12
    )(m3, e3, t1h, t1l)
    d2, full1_2, full2_2 = call(
        middle_kernel, "middle", [piece_shape, one, one],
        [SMEM] * 3 + [VMEM] * 9, [VMEM] * 3, halves_scratch(1),
        9 * 10**9, 10 * 2**20, vmem=24,
    )(*scalars, m2, full1_3, full2, t1h, t1l, t2h, t2l, within, across)
    r2 = exchange(d2, 2)
    d1, d3 = call(
        late_kernel, "late", [piece_shape] * 2, [SMEM] * 3 + [VMEM] * 7, [VMEM] * 2,
        halves_scratch(1) + [full_scratch(1)],
        7 * 10**9, 4 * 2**20, vmem=20,
    )(*scalars, full1_2, full1_3, full2, t2h, t2l, within, across)
    r1 = exchange(d1, 1)
    r3 = exchange(d3, 3)
    (result,) = call(
        rest_kernel, "rest", [((2, RING * QROWS, WIDTH), f32)], [SMEM] * 3 + [VMEM] * 4, [HBM],
        [pltpu.VMEM(*piece_shape), dma((1,))],
        3 * 10**9, 3 * 2**20, vmem=12,
    )(*scalars, full2, full2_2, within, across)

    for distances, pieces, flops in (((2,), (r2,), 10**11), ((1, 3), (r1, r3), 10**5)):
        (result,) = call(
            functools.partial(place_kernel, distances), "place", [(result.shape, f32)],
            [SMEM] + [VMEM] * len(pieces) + [HBM], [HBM], [dma((4 * len(pieces),))],
            flops, 2**21, {1 + len(pieces): 0},
        )(where, *pieces, result)
    return result[:, None]


def solution(mesh):
    return jax.shard_map(
        per_device,
        mesh=mesh,
        in_specs=(
            P(None, "grp", "beam", None),
            P(),
            P(),
            P(None, None, "beam"),
            P(None, None, "beam"),
        ),
        out_specs=P(None, "grp", "beam", None),
        check_vma=False,
    )
```
